128 devices in a mesh: dp: 8 (over z, core), tensor: 16 (over x, y).
Axes of the slice: x: 4, y: 4, z: 4, core: 2. Of those that a mesh axis runs over, the one named last changes fastest.
Arguments:
- hidden: bfloat16 [512, 8192], P('dp'), may hold values from -180 to 180
- weight: bfloat16 [8192, 114688], P(None, ('dp', 'tensor')), may hold values from -4 to 4
- ref_logits: bfloat16 [512, 114688], P(('dp', 'tensor')), may hold values from -867 to 867
- targets: int32 [512], replicated, may hold values from 0 to 114687
- sequence: int32 [512], replicated, may hold values from 0 to 15, never falling along the last dimension, each value on 1 to 64 neighbouring positions
- response: int32 [512], replicated, may hold values 0 or 1
Outputs:
- d_hidden: bfloat16 [512, 8192], P(('dp', 'tensor'))
- loss: float32 [], replicated
The draws below stay inside these ranges and needn't reach their ends.
Inputs may be any that keep to these rules, and one draw needn't show every extreme that they name: Sequence ids never fall along the tokens; each sequence has 1 to 64 tokens, the longest exactly 64; a sequence with an even id is the chosen response of a pair and the next id its rejected response.
All inputs are finite; a program needn't handle non-finite values.
Results may differ from the reference program's by a relative error of at most 0.012.
Values may be sent and summed in bfloat16 or wider, within the bound.
No kernel may reach another device: no remote copies, remote signals or barrier semaphores. Data moves between devices by JAX's collectives and lax.ppermute only.
A program may use at most 128 MiB of HBM per device.

```python
import math
import jax
import jax.numpy as jnp
import numpy as np
from jax import lax

D = 8192
VOCAB = 114688
SEQ_GRP = 2
TOKENS = 512
SEQS = 16
MOST_LEN = 64
N_DP = 8


def shared_factors(key, mild_low, mild_high, strong_low, strong_high):
    row_key = jax.random.fold_in(key, 101)
    levels = jax.random.uniform(jax.random.fold_in(row_key, 1), (TOKENS,), jnp.float32, 2.0, 3.0)
    flipped = jax.random.bernoulli(jax.random.fold_in(row_key, 2), 0.5, (TOKENS,))
    drawn_scale = jax.random.uniform(jax.random.fold_in(row_key, 3), (TOKENS,), jnp.float32, mild_low, mild_high)
    strong_scale = jax.random.uniform(jax.random.fold_in(row_key, 4), (TOKENS,), jnp.float32, strong_low, strong_high)
    picked = jnp.arange(TOKENS) % 16 == 0
    row_factor = jnp.where(flipped, 1.0, -1.0) * levels * jnp.where(picked, strong_scale, drawn_scale)
    column = jnp.clip(jax.random.normal(jax.random.fold_in(key, 102), (VOCAB,), jnp.float32), -4.0, 4.0)
    row_factor = row_factor.astype(jnp.bfloat16).astype(jnp.float32)
    column = column.astype(jnp.bfloat16).astype(jnp.float32)
    return (row_factor, column)


def draw_hidden(key, part):
    row_factor, column = shared_factors(key, 1.0, 1.0, 1.0, 1.0)
    key = jax.random.fold_in(key, 11)
    rest = jnp.clip(jax.random.normal(key, (TOKENS, D), jnp.float32), -6.0, 6.0) * 0.5
    values = jnp.where(jnp.arange(D)[None, :] == 0, row_factor[:, None], rest)
    return values.astype(jnp.bfloat16)


def draw_weight(key, part):
    row_factor, column = shared_factors(key, 1.0, 1.0, 1.0, 1.0)
    key = jax.random.fold_in(key, 17)
    rest = jnp.clip(jax.random.normal(key, (D, VOCAB), jnp.float32), -6.0, 6.0) / jnp.sqrt(jnp.float32(D))
    values = jnp.where(jnp.arange(D)[:, None] == 0, column[None, :], rest)
    return values.astype(jnp.bfloat16)


def draw_ref_logits(key, part):
    row_factor, column = shared_factors(key, 1.0, 1.0, 1.0, 1.0)
    key = jax.random.fold_in(key, 23)
    noise = jnp.clip(jax.random.normal(key, (TOKENS, VOCAB), jnp.float32), -6.0, 6.0) * 0.5
    values = 1.2 * (row_factor[:, None] * column[None, :]) + noise
    return values.astype(jnp.bfloat16)


def place_ends(drawn, stream_key, least, top_value):
    extent = drawn.shape
    spot = [jax.random.randint(jax.random.fold_in(stream_key, axis), (), 0, extent[axis]) for axis in range(len(extent))]
    drawn = drawn.at[tuple(spot)].set(least)
    longest = extent.index(max(extent))
    spot[longest] = (spot[longest] + 1) % extent[longest]
    return drawn.at[tuple(spot)].set(top_value)


def length_profile(count, total, bound, slope):
    weights = [(1 << 20) // math.isqrt(rank ** slope) + 1 for rank in range(2, count + 1)]
    spare, counts = total - bound - (count - 1), [1] * (count - 1)
    while spare > 0:
        free = [i for i in range(count - 1) if counts[i] < bound]
        mass, remaining = sum([weights[i] for i in free]), spare
        for i in free:
            extra = min(bound - counts[i], max(1, remaining * weights[i] // mass), spare)
            counts[i] = counts[i] + extra
            spare = spare - extra
    return np.array([bound] + counts)


def uneven_parts(key, number_of, total, reach, lean):
    if number_of == 2:
        one = jax.random.randint(key, (), max(1, total - reach), min(reach, total - 1) + 1)
        return jnp.stack([one, total - one])
    tallies = jnp.asarray(length_profile(number_of, total, reach, lean), jnp.int32)
    pairs = (number_of - 1) // 2
    giver, taker = tallies[1:1 + 2 * pairs:2], tallies[2:2 + 2 * pairs:2]
    room = jnp.minimum(giver - 1, reach - taker)
    moved = jax.random.randint(jax.random.fold_in(key, 1), (pairs,), 0, 1 << 20) % (room + 1)
    tallies = tallies.at[1:1 + 2 * pairs:2].set(giver - moved).at[2:2 + 2 * pairs:2].set(taker + moved)
    return tallies[jax.random.permutation(jax.random.fold_in(key, 2), number_of)]


def setup_inputs(seed: int = 0) -> dict:
    arg_keys = jax.random.split(jax.random.key(seed), 7)
    return {
        "hidden": draw_hidden(jax.random.fold_in(arg_keys[6], 71), 0),
        "weight": draw_weight(jax.random.fold_in(arg_keys[6], 71), 0),
        "ref_logits": draw_ref_logits(jax.random.fold_in(arg_keys[6], 71), 0),
        "targets": place_ends(jax.random.randint(arg_keys[3], (TOKENS,), 0, VOCAB), jax.random.fold_in(arg_keys[3], 1), 0, VOCAB - 1).astype(jnp.int32),
        "sequence": jnp.searchsorted(jnp.cumsum(uneven_parts(arg_keys[4], SEQS, TOKENS, MOST_LEN, 0)), jnp.arange(TOKENS), side="right").astype(jnp.int32),
        "response": place_ends((jax.random.randint(arg_keys[5], (TOKENS,), 0, 4) < 3).astype(jnp.int32), jax.random.fold_in(arg_keys[5], 1), 0, 1),
    }


BETA = 0.05
KL_WEIGHT = 0.1
LOSS_SCALE = 1024.0


def objective_parts(policy, refer, target_hit, stats, sequence, response, n_seq):
    peak, total, cross, ref_peak, ref_total, picked, ref_picked = stats
    log_total = peak + jnp.log(total)
    ref_log_total = ref_peak + jnp.log(ref_total)
    diverge = cross / total - log_total + ref_log_total
    maskf = response.astype(jnp.float32)
    delta = maskf * ((picked - log_total) - (ref_picked - ref_log_total))
    member = (sequence[:, None] == jnp.arange(n_seq, dtype=jnp.int32)[None, :]).astype(jnp.float32)
    seq_sums = jnp.sum(member * delta[:, None], axis=0)
    margin = BETA * (seq_sums[0::2] - seq_sums[1::2])
    losses = jax.nn.softplus(-margin)
    pull = BETA * jax.nn.sigmoid(-margin)
    seq_grad = jnp.stack([-pull, pull], axis=1).reshape(-1)
    token_grad = jnp.sum(member * seq_grad[None, :], axis=1)
    loss = (jnp.sum(losses) + KL_WEIGHT * jnp.sum(maskf * diverge)) / policy.shape[0]
    probs = jnp.exp(policy - log_total[:, None])
    inner = token_grad[:, None] * (target_hit - probs) + KL_WEIGHT * probs * ((policy - refer) - (log_total - ref_log_total)[:, None] - diverge[:, None])
    grad = LOSS_SCALE * maskf[:, None] * inner
    return grad.astype(jnp.bfloat16), loss


def reference(hidden, weight, ref_logits, targets, sequence, response):
    policy = jnp.dot(hidden, weight, preferred_element_type=jnp.float32)
    refer = ref_logits.astype(jnp.float32)
    columns = jnp.arange(VOCAB, dtype=jnp.int32)
    target_hit = (targets[:, None] == columns[None, :]).astype(jnp.float32)
    peak = jnp.max(policy, axis=1)
    scaled = jnp.exp(policy - peak[:, None])
    total = jnp.sum(scaled, axis=1)
    cross = jnp.sum(scaled * (policy - refer), axis=1)
    ref_peak = jnp.max(refer, axis=1)
    ref_total = jnp.sum(jnp.exp(refer - ref_peak[:, None]), axis=1)
    picked = jnp.sum(target_hit * policy, axis=1)
    ref_picked = jnp.sum(target_hit * refer, axis=1)
    stats = (peak, total, cross, ref_peak, ref_total, picked, ref_picked)
    grad, loss = objective_parts(policy, refer, target_hit, stats, sequence, response, SEQ_GRP * N_DP)
    d_hidden = lax.dot_general(grad, weight, (((1,), (1,)), ((), ())), preferred_element_type=jnp.float32)
    return d_hidden.astype(jnp.bfloat16), loss
```

```python
import functools

import jax
import jax.numpy as jnp
from jax import lax
from jax.experimental import pallas as pl
from jax.experimental.pallas import tpu as pltpu
from jax.sharding import PartitionSpec as P

BETA = 0.05
KL_WEIGHT = 0.1
LOSS_SCALE = 1024.0
BF16 = jnp.bfloat16
F32 = jnp.float32

RING = 4
CORES = 2
CHIPS = RING * RING


def swap_tensor(value, offset):
    return lax.ppermute(value, "tensor", [(i, i ^ offset) for i in range(CHIPS)])


def swap_z(value, offset):
    return lax.ppermute(value, "dp", [(i, i ^ (offset * CORES)) for i in range(RING * CORES)])


def swap_core(value):
    return lax.ppermute(value, "dp", [(i, i ^ 1) for i in range(RING * CORES)])


def any_spec():
    return pl.BlockSpec(memory_space=pl.ANY)


def params(mib):
    return pltpu.CompilerParams(vmem_limit_bytes=mib * 1024 * 1024)


def place_of(first, second):
    b, e = first >> 1, second >> 1
    return ((first & 1) ^ b) + 2 * b + 4 * ((second & 1) ^ e) + 8 * e


def where_am_i():
    dp, t = lax.axis_index("dp"), lax.axis_index("tensor")
    return dp & 1, t >> 2, t & 3, dp >> 1


def logits_body(*refs):
    (mine, theirs), near, gathered, weight, policy_ref = refs[:2], refs[2:6], refs[6:14], refs[14], refs[15]
    states, pieces, slabs, sems = refs[16:]
    rows = mine.shape[0]
    half = near[0].shape[1]
    depth = half // RING
    width = half // CHIPS
    core, x, y, z = where_am_i()

    def rows_of(dz, side):
        start = (z ^ dz) * (2 * rows) + (core ^ side) * rows
        return pl.ds(pl.multiple_of(start, rows), rows)

    loads = [
        pltpu.make_async_copy(ref, pieces.at[i // 2, pl.ds(8 * (i % 2), 8)], sems.at[i]) for i, ref in enumerate(gathered)
    ]
    slices = []
    for k in range(2 * RING):
        far = k // RING
        here = pl.ds(k * depth, depth)
        there = pl.ds(pl.multiple_of((core ^ far) * half + (k % RING) * depth, depth), depth)
        within = pl.ds((k % RING) * depth, depth)
        moves = [
            (mine.at[:, there], states.at[rows_of(0, 0), here]),
            (theirs.at[:, there], states.at[rows_of(0, 1), here]),
        ]
        for dz, block in ((1, near[2 * far]), (3, near[2 * far + 1])):
            for side in range(CORES):
                moves.append((block.at[pl.ds(side * rows, rows), within], states.at[rows_of(dz, side ^ far), here]))
        moves.append((weight.at[there], slabs.at[k]))
        slices.append([pltpu.make_async_copy(a, b, sems.at[8 + 7 * k + i]) for i, (a, b) in enumerate(moves)])
    for copy in loads[:4] + slices[0] + loads[4:]:
        copy.start()
    for k in range(1, 2 * RING):
        for copy in slices[k]:
            copy.start()
    for far in range(2):
        for copy in loads[4 * far : 4 * far + 4]:
            copy.wait()
        for k in range(RING):
            for j in range(RING):
                at = pl.ds(far * half + (k * RING + j) * width, width)
                states[rows_of(2, far), at] = pieces[2 * far, place_of(y ^ j, x ^ k)]
                states[rows_of(2, 1 - far), at] = pieces[2 * far + 1, place_of(x ^ k, y ^ j)]
        for k in range(far * RING, (far + 1) * RING):
            for copy in slices[k]:
                copy.wait()
            product = jnp.dot(states[:, k * depth : (k + 1) * depth], slabs[k], preferred_element_type=F32)
            policy_ref[...] = product if k == 0 else policy_ref[...] + product


def policy_logits(mine, theirs, near, gathered, weight):
    rows, half = mine.shape[0], near[0].shape[1]
    tokens = rows * CORES * RING
    cols = weight.shape[1]
    width = half // CHIPS
    return pl.pallas_call(
        logits_body,
        out_shape=jax.ShapeDtypeStruct((tokens, cols), F32),
        in_specs=[any_spec()] * 15,
        out_specs=pl.BlockSpec(memory_space=pltpu.VMEM),
        scratch_shapes=[
            pltpu.VMEM((tokens, 2 * half), BF16),
            pltpu.VMEM((4, CHIPS, rows, width), BF16),
            pltpu.VMEM((2 * RING, half // RING, cols), BF16),
            pltpu.SemaphoreType.DMA((8 + 7 * 2 * RING,)),
        ],
        compiler_params=params(52),
        cost_estimate=pl.CostEstimate(
            flops=4 * tokens * half * cols, bytes_accessed=4 * half * (cols + tokens) + 4 * tokens * cols, transcendentals=0
        ),
        name="policy_logits",
    )(mine, theirs, *near, *gathered, weight)


def stats_body(targets_ref, policy_ref, refer_ref, stats_ref):
    rows, cols = policy_ref.shape
    core, x, y, z = where_am_i()
    start_col = (((z * CORES + core) * RING + x) * RING + y) * cols
    local = targets_ref[...].reshape(1, rows) - start_col
    local = jnp.where((local >= 0) & (local < cols), local, -1).astype(F32)
    local = jnp.broadcast_to(local, (128, rows)).T[:, 0:1].astype(jnp.int32)
    policy = policy_ref[...]
    refer = refer_ref[...].astype(F32)
    hit = lax.broadcasted_iota(jnp.int32, (rows, cols), 1) == local
    peak = jnp.max(policy, axis=1, keepdims=True)
    scaled = jnp.exp(policy - peak)
    total = jnp.sum(scaled, axis=1, keepdims=True)
    cross = jnp.sum(scaled * (policy - refer), axis=1, keepdims=True)
    ref_peak = jnp.max(refer, axis=1, keepdims=True)
    ref_total = jnp.sum(jnp.exp(refer - ref_peak), axis=1, keepdims=True)
    picked = jnp.sum(jnp.where(hit, policy, 0.0), axis=1, keepdims=True)
    ref_picked = jnp.sum(jnp.where(hit, refer, 0.0), axis=1, keepdims=True)
    lane = lax.broadcasted_iota(jnp.int32, (rows, 128), 1)
    table = jnp.zeros((rows, 128), F32)
    for k, value in enumerate((peak, total, cross, ref_peak, ref_total, picked, ref_picked)):
        table = jnp.where(lane == k, value, table)
    stats_ref[...] = table.T[:8]


def row_stats(targets, policy, refer):
    tokens, cols = policy.shape
    step = 128
    return pl.pallas_call(
        stats_body,
        grid=(tokens // step,),
        out_shape=jax.ShapeDtypeStruct((8, tokens), F32),
        in_specs=[
            pl.BlockSpec((step,), lambda i: (i,)),
            pl.BlockSpec((step, cols), lambda i: (i, 0)),
            pl.BlockSpec((step, cols), lambda i: (i, 0)),
        ],
        out_specs=pl.BlockSpec((8, step), lambda i: (0, i)),
        compiler_params=params(24),
        cost_estimate=pl.CostEstimate(flops=20 * tokens * cols, bytes_accessed=6 * tokens * cols, transcendentals=2 * tokens * cols),
        name="row_stats",
    )(targets, policy, refer)


def merge(stats):
    table = jnp.stack(stats)
    peak = jnp.max(table[:, 0], axis=0)
    share = jnp.exp(table[:, 0] - peak)
    total = jnp.sum(share * table[:, 1], axis=0)
    cross = jnp.sum(share * table[:, 2], axis=0)
    ref_peak = jnp.max(table[:, 3], axis=0)
    ref_total = jnp.sum(jnp.exp(table[:, 3] - ref_peak) * table[:, 4], axis=0)
    picked = jnp.sum(table[:, 5], axis=0)
    ref_picked = jnp.sum(table[:, 6], axis=0)
    return jnp.stack([peak, total, cross, ref_peak, ref_total, picked, ref_picked, jnp.zeros_like(peak)])


def grad_body(n_seq, stats_ref, targets_ref, sequence_ref, response_ref, policy_ref, refer_ref, by_x_ref, by_y_ref, loss_ref):
    tokens, cols = policy_ref.shape
    core_here, x, y, z = where_am_i()
    start_col = (((z * CORES + core_here) * RING + x) * RING + y) * cols
    stats = stats_ref[...]
    peak, total, cross, ref_peak, ref_total, picked, ref_picked = [stats[k : k + 1] for k in range(7)]
    targets, sequence, response = [ref[...].reshape(1, tokens) for ref in (targets_ref, sequence_ref, response_ref)]
    log_total = peak + jnp.log(total)
    ref_log_total = ref_peak + jnp.log(ref_total)
    mean_gap = cross / total
    diverge = mean_gap - log_total + ref_log_total
    mask = response.astype(F32)
    delta = mask * ((picked - log_total) - (ref_picked - ref_log_total))
    ids = lax.broadcasted_iota(jnp.int32, (n_seq, tokens), 0)
    member = (ids == sequence).astype(F32)
    pair = lax.broadcasted_iota(jnp.int32, (n_seq // 2, tokens), 0)
    side = jnp.where(pair == sequence >> 1, jnp.where((sequence & 1) == 0, 1.0, -1.0), 0.0)
    margin = BETA * jnp.sum(side * delta, axis=1, keepdims=True)
    pull = BETA * jax.nn.sigmoid(-margin)
    token_grad = -jnp.sum(side * pull, axis=0, keepdims=True)
    losses = jnp.maximum(-margin, 0.0) + jnp.log1p(jnp.exp(-jnp.abs(margin)))
    objective = jnp.sum(losses) + KL_WEIGHT * jnp.sum(mask * diverge)
    loss_ref[...] = jnp.full(loss_ref.shape, objective / tokens, F32)

    lift = LOSS_SCALE * mask
    local = targets - start_col
    local = jnp.where((local >= 0) & (local < cols), local, -1).astype(F32)
    rows8 = lax.broadcasted_iota(jnp.int32, (128, tokens), 0)
    packed = jnp.zeros((128, tokens), F32)
    for k, value in enumerate((log_total, mean_gap, lift * token_grad, lift * KL_WEIGHT, local)):
        packed = jnp.where(rows8 == k, value, packed)
    packed = packed.T

    step = 128
    pieces = []
    for i in range(tokens // step):
        span = slice(i * step, (i + 1) * step)
        per_row = packed[span]
        policy = policy_ref[span, :]
        refer = refer_ref[span, :].astype(F32)
        column = lax.broadcasted_iota(jnp.int32, (step, cols), 1)
        hit = (column == per_row[:, 4:5].astype(jnp.int32)).astype(F32)
        probs = jnp.exp(policy - per_row[:, 0:1])
        grad = per_row[:, 2:3] * (hit - probs) + per_row[:, 3:4] * probs * ((policy - refer) - per_row[:, 1:2])
        pieces.append(grad.astype(BF16))
    grad = jnp.concatenate(pieces, axis=0)

    row = lax.broadcasted_iota(jnp.int32, (tokens, tokens), 0)
    token = lax.broadcasted_iota(jnp.int32, (tokens, tokens), 1)
    outer, inner, dz, core, t = row >> 7, (row >> 5) & 3, (row >> 3) & 3, (row >> 2) & 1, row & 3
    base = (z ^ dz) * 128 + core * 64 + t
    for ref, source in (
        (by_x_ref, base + (x ^ outer) * 16 + (y ^ inner) * 4),
        (by_y_ref, base + (x ^ inner) * 16 + (y ^ outer) * 4),
    ):
        pick = (token == source).astype(F32).astype(BF16)
        ref[...] = jnp.dot(pick, grad, preferred_element_type=F32).astype(BF16)


def logit_grads(stats, targets, sequence, response, policy, refer, n_seq):
    tokens, cols = policy.shape
    vmem = pl.BlockSpec(memory_space=pltpu.VMEM)
    return pl.pallas_call(
        functools.partial(grad_body, n_seq),
        out_shape=(
            jax.ShapeDtypeStruct((tokens, cols), BF16),
            jax.ShapeDtypeStruct((tokens, cols), BF16),
            jax.ShapeDtypeStruct((8, 128), F32),
        ),
        in_specs=[vmem] * 6,
        out_specs=(vmem, vmem, vmem),
        compiler_params=params(24),
        cost_estimate=pl.CostEstimate(flops=2 * tokens * tokens * cols, bytes_accessed=10 * tokens * cols, transcendentals=tokens * cols),
        name="logit_grads",
    )(stats, targets, sequence, response, policy, refer)


PARTS = ((True, 1), (True, 3), (False, 1), (False, 3))
SENDS = {1: (1, 2), 3: (3, 2)}
KEEPS = {1: (0, 3), 3: (0, 1)}


def hidden_body(own_x, other_x, own_y, other_y, own_weight, other_weight, *refs):
    outs, (grads, slabs, sems) = refs[:8], refs[8:]
    tokens, cols = own_x.shape
    core = lax.axis_index("dp") & 1
    half = own_weight.shape[0] // CORES
    depth = half // 4
    step = depth // 2
    loads = [
        pltpu.make_async_copy(ref, grads.at[i // 2, :, pl.ds((i % 2) * cols, cols)], sems.at[i])
        for i, ref in enumerate((own_x, other_x, own_y, other_y))
    ]
    fetches = []
    for i in range(8):
        rows = pl.ds(pl.multiple_of(core * half + i * step, step), step)
        fetches.append(
            [
                pltpu.make_async_copy(ref.at[rows], slabs.at[i, :, pl.ds(n * cols, cols)], sems.at[4 + 2 * i + n])
                for n, ref in enumerate((own_weight, other_weight))
            ]
        )
    for copy in loads[:2] + sum(fetches[:4], []) + loads[2:] + sum(fetches[4:], []):
        copy.start()
    quarter = tokens // RING
    for i in range(8):
        part = i // 2
        if i % 4 == 0:
            loads[i // 2].wait()
            loads[i // 2 + 1].wait()
        for copy in fetches[i]:
            copy.wait()
        product = lax.dot_general(
            grads[i // 4], slabs[i], (((1,), (1,)), ((), ())), preferred_element_type=F32
        ).astype(BF16)
        first = PARTS[part][1]
        for ref, order in ((outs[2 * part], SENDS[first]), (outs[2 * part + 1], KEEPS[first])):
            for k, source in enumerate(order):
                ref[k * quarter : (k + 1) * quarter, (i % 2) * step : (i % 2 + 1) * step] = product[
                    source * quarter : (source + 1) * quarter
                ]


def hidden_parts(grads, weight, other_weight):
    tokens, cols = grads[0].shape
    depth = weight.shape[0] // CORES // 4
    vmem = pl.BlockSpec(memory_space=pltpu.VMEM)
    return pl.pallas_call(
        hidden_body,
        out_shape=(jax.ShapeDtypeStruct((tokens // 2, depth), BF16),) * 8,
        in_specs=[any_spec()] * 6,
        out_specs=(vmem,) * 8,
        scratch_shapes=[
            pltpu.VMEM((2, tokens, CORES * cols), BF16),
            pltpu.VMEM((8, depth // 2, CORES * cols), BF16),
            pltpu.SemaphoreType.DMA((20,)),
        ],
        compiler_params=params(52),
        cost_estimate=pl.CostEstimate(
            flops=16 * tokens * depth * cols, bytes_accessed=16 * cols * (tokens + depth) + 8 * tokens * depth, transcendentals=0
        ),
        name="hidden_parts",
    )(*grads, weight, other_weight)


def add(*terms):
    total = terms[0].astype(F32)
    for term in terms[1:]:
        total = total + term.astype(F32)
    return total


def shards(hidden, weight, ref_logits, targets, sequence, response):
    rows, width = hidden.shape
    cols = weight.shape[1]
    half = width // CORES
    piece = half // CHIPS
    dp, t = lax.axis_index("dp"), lax.axis_index("tensor")
    z, core = dp // CORES, dp % CORES
    x, y = t // RING, t % RING

    theirs = swap_core(hidden)
    sent_weight, theirs = lax.optimization_barrier((weight, theirs))
    other_weight = swap_core(sent_weight)
    across = jnp.concatenate(
        [lax.dynamic_slice_in_dim(a, core * half + t * piece, piece, axis=1) for a in (hidden, theirs)], axis=0
    )
    across = swap_z(across, 2)
    sent, across = lax.optimization_barrier(((hidden, theirs), across))
    pair = jnp.concatenate([lax.dynamic_slice_in_dim(a, core * half, half, axis=1) for a in sent], axis=0)
    near = [swap_z(pair, 1), swap_z(pair, 3)]
    by_x, by_y = across[None, :rows], across[None, rows:]
    for step_x, step_y in ((1, 4), (3, 12), (4, 1)):
        by_x, by_y = (
            jnp.concatenate([by_x, swap_tensor(by_x, step_x)], axis=0),
            jnp.concatenate([by_y, swap_tensor(by_y, step_y)], axis=0),
        )
    gathered = [by_x, swap_tensor(by_x, 12), by_y, swap_tensor(by_y, 3)]
    near += [swap_core(a) for a in near]

    ref_logits, gathered = lax.optimization_barrier((ref_logits, gathered))
    refer = lax.all_to_all(
        ref_logits.reshape(ref_logits.shape[0], -1, cols), ("dp", "tensor"), split_axis=1, concat_axis=0
    )

    swapped = [swap_core(a) for a in gathered]
    policy = policy_logits(hidden, theirs, near, gathered + swapped, weight)
    refer, policy = lax.optimization_barrier((refer, policy))
    refer = refer.reshape(policy.shape)
    stats = row_stats(targets, policy, refer)

    for send, steps in (
        (swap_tensor, (1, 2, 3)),
        (swap_tensor, (4, 8, 12)),
        (swap_z, (1, 2, 3)),
    ):
        stats = merge([stats] + [send(stats, o) for o in steps])
    stats = merge([stats, swap_core(stats)])

    grad_x, grad_y, loss = logit_grads(stats, targets, sequence, response, policy, refer, 2 * RING * CORES)
    grads = (grad_x, swap_core(grad_x), grad_y, swap_core(grad_y))

    sums = {4: [], 1: []}
    products = hidden_parts(grads, weight, other_weight)
    for part, (along_x, first) in enumerate(PARTS):
        send, keep = products[2 * part], products[2 * part + 1]
        axis = RING if along_x else 1
        got = swap_tensor(send, axis * first)
        n = keep.shape[0] // 2
        more = swap_tensor(add(keep[n:], got[n:]).astype(BF16), axis * (RING - first))
        sums[axis].append(add(keep[:n], got[:n], more).astype(BF16))
    ends = []
    for axis, cross in ((4, 1), (1, 4)):
        block = jnp.concatenate(sums[axis], axis=1)
        block = block.reshape(RING, block.shape[0] // RING, -1)
        ends.append(add(block[0], *[swap_tensor(block[k], cross * k) for k in (2, 1, 3)]).astype(BF16))
    ends = jnp.concatenate(ends, axis=1).reshape(RING, CORES * RING, half)
    d_half = add(ends[0], *[swap_z(ends[k], k) for k in (2, 1, 3)]).astype(BF16).reshape(CORES, RING, half)
    own_rows = lax.dynamic_index_in_dim(d_half, core, 0, keepdims=False)
    got_rows = swap_core(lax.dynamic_index_in_dim(d_half, 1 - core, 0, keepdims=False))
    d_hidden = jnp.where(
        core == 0, jnp.concatenate([own_rows, got_rows], axis=1), jnp.concatenate([got_rows, own_rows], axis=1)
    )
    return d_hidden, loss[0, 0]


def solution(mesh):
    in_specs = (P("dp", None), P(None, ("dp", "tensor")), P(("dp", "tensor"), None), P(), P(), P())
    out_specs = (P(("dp", "tensor"), None), P())
    return jax.shard_map(shards, mesh=mesh, in_specs=in_specs, out_specs=out_specs, check_vma=False)
```

```python
import functools

import jax
import jax.numpy as jnp
from jax import lax
from jax.experimental import pallas as pl
from jax.experimental.pallas import tpu as pltpu
from jax.sharding import PartitionSpec as P

BETA = 0.05
KL_WEIGHT = 0.1
LOSS_SCALE = 1024.0
BF16 = jnp.bfloat16
F32 = jnp.float32

RING = 4
CORES = 2
CHIPS = RING * RING


def swap_tensor(value, offset):
    return lax.ppermute(value, "tensor", [(i, i ^ offset) for i in range(CHIPS)])


def swap_z(value, offset):
    return lax.ppermute(value, "dp", [(i, i ^ (offset * CORES)) for i in range(RING * CORES)])


def swap_core(value):
    return lax.ppermute(value, "dp", [(i, i ^ 1) for i in range(RING * CORES)])


def any_spec():
    return pl.BlockSpec(memory_space=pl.ANY)


def params(mib):
    return pltpu.CompilerParams(vmem_limit_bytes=mib * 1024 * 1024)


def place_of(first, second):
    b, e = first >> 1, second >> 1
    return ((first & 1) ^ b) + 2 * b + 4 * ((second & 1) ^ e) + 8 * e


def where_am_i():
    dp, t = lax.axis_index("dp"), lax.axis_index("tensor")
    return dp & 1, t >> 2, t & 3, dp >> 1


def logits_body(*refs):
    (mine, theirs), near, gathered, weight, policy_ref = refs[:2], refs[2:6], refs[6:14], refs[14], refs[15]
    states, pieces, slabs, sems = refs[16:]
    rows, width = mine.shape
    depth = width // (2 * RING)
    span = width // CHIPS
    core, x, y, z = where_am_i()

    def rows_of(dz, side, start=0, size=rows):
        start = (z ^ dz) * (2 * rows) + (core ^ side) * rows + start
        return pl.ds(pl.multiple_of(start, size), size)

    loads = [
        pltpu.make_async_copy(ref, pieces.at[i // 2, pl.ds(8 * (i % 2), 8)], sems.at[i]) for i, ref in enumerate(gathered)
    ]
    blocks = [(0, 0, mine), (0, 1, theirs), (1, 0, near[0]), (3, 0, near[1]), (1, 1, near[2]), (3, 1, near[3])]
    slices = []
    for k in range(2 * RING):
        here = pl.ds(k * depth, depth)
        moves = [(block.at[:, here], states.at[rows_of(dz, side), here]) for dz, side, block in blocks]
        moves.append((weight.at[here], slabs.at[k]))
        slices.append([pltpu.make_async_copy(a, b, sems.at[8 + 7 * k + i]) for i, (a, b) in enumerate(moves)])
    for copy in loads + slices[0]:
        copy.start()
    for k in range(1, 2 * RING):
        for copy in slices[k]:
            copy.start()
    for copy in loads:
        copy.wait()
    for i in range(CHIPS):
        dx, dy = x ^ (i // RING), y ^ (i % RING)
        at = pl.ds(i * span, span)
        for side in range(CORES):
            states[rows_of(2, side, 0, rows // 2), at] = pieces[2 * side, place_of(dy, dx)]
            states[rows_of(2, side, rows // 2, rows // 2), at] = pieces[2 * side + 1, place_of(dx, dy)]
    for k in range(2 * RING):
        for copy in slices[k]:
            copy.wait()
        product = jnp.dot(states[:, k * depth : (k + 1) * depth], slabs[k], preferred_element_type=F32)
        policy_ref[...] = product if k == 0 else policy_ref[...] + product


def policy_logits(mine, theirs, near, gathered, weight):
    rows, width = mine.shape
    tokens = rows * CORES * RING
    cols = weight.shape[1]
    return pl.pallas_call(
        logits_body,
        out_shape=jax.ShapeDtypeStruct((tokens, cols), F32),
        in_specs=[any_spec()] * 15,
        out_specs=pl.BlockSpec(memory_space=pltpu.VMEM),
        scratch_shapes=[
            pltpu.VMEM((tokens, width), BF16),
            pltpu.VMEM((4, CHIPS, rows // 2, width // CHIPS), BF16),
            pltpu.VMEM((2 * RING, width // (2 * RING), cols), BF16),
            pltpu.SemaphoreType.DMA((8 + 7 * 2 * RING,)),
        ],
        compiler_params=params(52),
        cost_estimate=pl.CostEstimate(
            flops=2 * tokens * width * cols, bytes_accessed=2 * width * (cols + tokens) + 4 * tokens * cols, transcendentals=0
        ),
        name="policy_logits",
    )(mine, theirs, *near, *gathered, weight)


def in_token_order(refer):
    shape = (refer.shape[0], refer.shape[0])
    row, source = lax.broadcasted_iota(jnp.int32, shape, 0), lax.broadcasted_iota(jnp.int32, shape, 1)
    wanted = ((row >> 2) & 15) * 8 + (row >> 6) * 4 + (row & 3)
    return jnp.dot((source == wanted).astype(F32).astype(BF16), refer, preferred_element_type=F32)


def stats_body(targets_ref, policy_ref, refer_ref, stats_ref):
    rows, cols = policy_ref.shape
    core, x, y, z = where_am_i()
    start_col = (((z * CORES + core) * RING + x) * RING + y) * cols
    local = targets_ref[...].reshape(1, rows) - start_col
    local = jnp.where((local >= 0) & (local < cols), local, -1).astype(F32)
    local = jnp.broadcast_to(local, (128, rows)).T[:, 0:1].astype(jnp.int32)
    policy = policy_ref[...]
    refer = in_token_order(refer_ref[...])
    hit = lax.broadcasted_iota(jnp.int32, (rows, cols), 1) == local
    peak = jnp.max(policy, axis=1, keepdims=True)
    scaled = jnp.exp(policy - peak)
    total = jnp.sum(scaled, axis=1, keepdims=True)
    cross = jnp.sum(scaled * (policy - refer), axis=1, keepdims=True)
    ref_peak = jnp.max(refer, axis=1, keepdims=True)
    ref_total = jnp.sum(jnp.exp(refer - ref_peak), axis=1, keepdims=True)
    picked = jnp.sum(jnp.where(hit, policy, 0.0), axis=1, keepdims=True)
    ref_picked = jnp.sum(jnp.where(hit, refer, 0.0), axis=1, keepdims=True)
    lane = lax.broadcasted_iota(jnp.int32, (rows, 128), 1)
    table = jnp.zeros((rows, 128), F32)
    for k, value in enumerate((peak, total, cross, ref_peak, ref_total, picked, ref_picked)):
        table = jnp.where(lane == k, value, table)
    stats_ref[...] = table.T[:8]


def row_stats(targets, policy, refer):
    tokens, cols = policy.shape
    step = 128
    return pl.pallas_call(
        stats_body,
        grid=(tokens // step,),
        out_shape=jax.ShapeDtypeStruct((8, tokens), F32),
        in_specs=[
            pl.BlockSpec((step,), lambda i: (i,)),
            pl.BlockSpec((step, cols), lambda i: (i, 0)),
            pl.BlockSpec((step, cols), lambda i: (i, 0)),
        ],
        out_specs=pl.BlockSpec((8, step), lambda i: (0, i)),
        compiler_params=params(24),
        cost_estimate=pl.CostEstimate(flops=20 * tokens * cols, bytes_accessed=6 * tokens * cols, transcendentals=2 * tokens * cols),
        name="row_stats",
    )(targets, policy, refer)


def merge(stats):
    table = jnp.stack(stats)
    peak = jnp.max(table[:, 0], axis=0)
    share = jnp.exp(table[:, 0] - peak)
    total = jnp.sum(share * table[:, 1], axis=0)
    cross = jnp.sum(share * table[:, 2], axis=0)
    ref_peak = jnp.max(table[:, 3], axis=0)
    ref_total = jnp.sum(jnp.exp(table[:, 3] - ref_peak) * table[:, 4], axis=0)
    picked = jnp.sum(table[:, 5], axis=0)
    ref_picked = jnp.sum(table[:, 6], axis=0)
    return jnp.stack([peak, total, cross, ref_peak, ref_total, picked, ref_picked, jnp.zeros_like(peak)])


def grad_body(n_seq, stats_ref, targets_ref, sequence_ref, response_ref, policy_ref, refer_ref, grad_ref, loss_ref):
    tokens, cols = policy_ref.shape
    core_here, x, y, z = where_am_i()
    start_col = (((z * CORES + core_here) * RING + x) * RING + y) * cols
    stats = stats_ref[...]
    peak, total, cross, ref_peak, ref_total, picked, ref_picked = [stats[k : k + 1] for k in range(7)]
    targets, sequence, response = [ref[...].reshape(1, tokens) for ref in (targets_ref, sequence_ref, response_ref)]
    log_total = peak + jnp.log(total)
    ref_log_total = ref_peak + jnp.log(ref_total)
    mean_gap = cross / total
    diverge = mean_gap - log_total + ref_log_total
    mask = response.astype(F32)
    delta = mask * ((picked - log_total) - (ref_picked - ref_log_total))
    ids = lax.broadcasted_iota(jnp.int32, (n_seq, tokens), 0)
    member = (ids == sequence).astype(F32)
    pair = lax.broadcasted_iota(jnp.int32, (n_seq // 2, tokens), 0)
    side = jnp.where(pair == sequence >> 1, jnp.where((sequence & 1) == 0, 1.0, -1.0), 0.0)
    margin = BETA * jnp.sum(side * delta, axis=1, keepdims=True)
    pull = BETA * jax.nn.sigmoid(-margin)
    token_grad = -jnp.sum(side * pull, axis=0, keepdims=True)
    losses = jnp.maximum(-margin, 0.0) + jnp.log1p(jnp.exp(-jnp.abs(margin)))
    objective = jnp.sum(losses) + KL_WEIGHT * jnp.sum(mask * diverge)
    loss_ref[...] = jnp.full(loss_ref.shape, objective / tokens, F32)

    lift = LOSS_SCALE * mask
    local = targets - start_col
    local = jnp.where((local >= 0) & (local < cols), local, -1).astype(F32)
    rows8 = lax.broadcasted_iota(jnp.int32, (128, tokens), 0)
    packed = jnp.zeros((128, tokens), F32)
    for k, value in enumerate((log_total, mean_gap, lift * token_grad, lift * KL_WEIGHT, local)):
        packed = jnp.where(rows8 == k, value, packed)
    packed = packed.T

    step = 128
    pieces = []
    for i in range(tokens // step):
        span = slice(i * step, (i + 1) * step)
        per_row = packed[span]
        policy = policy_ref[span, :]
        refer = in_token_order(refer_ref[span, :])
        column = lax.broadcasted_iota(jnp.int32, (step, cols), 1)
        hit = (column == per_row[:, 4:5].astype(jnp.int32)).astype(F32)
        probs = jnp.exp(policy - per_row[:, 0:1])
        grad = per_row[:, 2:3] * (hit - probs) + per_row[:, 3:4] * probs * ((policy - refer) - per_row[:, 1:2])
        pieces.append(grad.astype(BF16))
    grad = jnp.concatenate(pieces, axis=0)

    row = lax.broadcasted_iota(jnp.int32, (tokens, tokens), 0)
    token = lax.broadcasted_iota(jnp.int32, (tokens, tokens), 1)
    dx, dy, dz, core, t = row >> 7, (row >> 5) & 3, (row >> 3) & 3, (row >> 2) & 1, row & 3
    source = (z ^ dz) * 128 + core * 64 + (x ^ dx) * 16 + (y ^ dy) * 4 + t
    pick = (token == source).astype(F32).astype(BF16)
    grad_ref[...] = jnp.dot(pick, grad, preferred_element_type=F32).astype(BF16)


def logit_grads(stats, targets, sequence, response, policy, refer, n_seq):
    tokens, cols = policy.shape
    vmem = pl.BlockSpec(memory_space=pltpu.VMEM)
    return pl.pallas_call(
        functools.partial(grad_body, n_seq),
        out_shape=(
            jax.ShapeDtypeStruct((tokens, cols), BF16),
            jax.ShapeDtypeStruct((8, 128), F32),
        ),
        in_specs=[vmem] * 6,
        out_specs=(vmem, vmem),
        compiler_params=params(24),
        cost_estimate=pl.CostEstimate(flops=2 * tokens * tokens * cols, bytes_accessed=10 * tokens * cols, transcendentals=tokens * cols),
        name="logit_grads",
    )(stats, targets, sequence, response, policy, refer)


PARTS = ((True, 1), (True, 3), (False, 1), (False, 3))
SENDS = {1: (1, 2), 3: (3, 2)}
KEEPS = {1: (0, 3), 3: (0, 1)}


def hidden_body(own_grad, other_grad, own_weight, other_weight, *refs):
    outs, (grads, slabs, results, sems) = refs[:8], refs[8:]
    tokens, cols = own_grad.shape
    core = lax.axis_index("dp") & 1
    half = own_weight.shape[0] // CORES
    depth = half // 4
    step = depth // 2
    loads = [
        pltpu.make_async_copy(ref, grads.at[:, pl.ds(i * cols, cols)], sems.at[i])
        for i, ref in enumerate((own_grad, other_grad))
    ]
    fetches = []
    for i in range(8):
        rows = pl.ds(pl.multiple_of(core * half + i * step, step), step)
        fetches.append(
            [
                pltpu.make_async_copy(ref.at[rows], slabs.at[i, :, pl.ds(n * cols, cols)], sems.at[2 + 2 * i + n])
                for n, ref in enumerate((own_weight, other_weight))
            ]
        )
    stores = [pltpu.make_async_copy(results.at[i], outs[i], sems.at[18 + i]) for i in range(8)]
    for copy in loads + sum(fetches, []):
        copy.start()
    for copy in loads:
        copy.wait()
    unit = tokens // CHIPS
    for i in range(8):
        part = i // 2
        along_x, first = PARTS[part]
        for copy in fetches[i]:
            copy.wait()
        product = lax.dot_general(grads[...], slabs[i], (((1,), (1,)), ((), ())), preferred_element_type=F32).astype(BF16)
        for n, order in ((2 * part, SENDS[first]), (2 * part + 1, KEEPS[first])):
            for k, outer in enumerate(order):
                for inner in range(RING):
                    source = (outer * RING + inner) if along_x else (inner * RING + outer)
                    there = (k * RING + inner) * unit
                    results[n, there : there + unit, (i % 2) * step : (i % 2 + 1) * step] = product[
                        source * unit : (source + 1) * unit
                    ]
        if i % 2 == 1:
            stores[2 * part].start()
            stores[2 * part + 1].start()
    for copy in stores:
        copy.wait()


def hidden_parts(own_grad, other_grad, weight, other_weight):
    tokens, cols = own_grad.shape
    depth = weight.shape[0] // CORES // 4
    return pl.pallas_call(
        hidden_body,
        out_shape=(jax.ShapeDtypeStruct((tokens // 2, depth), BF16),) * 8,
        in_specs=[any_spec()] * 4,
        out_specs=(any_spec(),) * 8,
        scratch_shapes=[
            pltpu.VMEM((tokens, CORES * cols), BF16),
            pltpu.VMEM((8, depth // 2, CORES * cols), BF16),
            pltpu.VMEM((8, tokens // 2, depth), BF16),
            pltpu.SemaphoreType.DMA((26,)),
        ],
        compiler_params=params(50),
        cost_estimate=pl.CostEstimate(
            flops=16 * tokens * depth * cols, bytes_accessed=16 * cols * (tokens + depth) + 8 * tokens * depth, transcendentals=0
        ),
        name="hidden_parts",
    )(own_grad, other_grad, weight, other_weight)


def add(*terms):
    total = terms[0].astype(F32)
    for term in terms[1:]:
        total = total + term.astype(F32)
    return total


def shards(hidden, weight, ref_logits, targets, sequence, response):
    rows, width = hidden.shape
    cols = weight.shape[1]
    half = width // CORES
    dp, t = lax.axis_index("dp"), lax.axis_index("tensor")
    z, core = dp // CORES, dp % CORES
    x, y = t // RING, t % RING

    piece = width // CHIPS
    across = swap_z(lax.dynamic_slice_in_dim(hidden, t * piece, piece, axis=1), 2)
    sent, across = lax.optimization_barrier((hidden, across))
    near = [swap_z(sent, 1), swap_z(sent, 3)]
    other_weight = swap_core(weight)
    theirs = swap_core(hidden)
    ref_logits = ref_logits.reshape(RING, RING, CORES, CHIPS, cols)
    ref_own, ref_other = [
        lax.dynamic_index_in_dim(ref_logits, c, 2, keepdims=False).transpose(1, 2, 0, 3).reshape(RING * CHIPS, RING, cols)
        for c in (core, 1 - core)
    ]
    ref_other = swap_core(ref_other)
    ref_both = jnp.where(
        core == 0, jnp.concatenate([ref_own, ref_other], axis=1), jnp.concatenate([ref_other, ref_own], axis=1)
    )
    by_x, by_y = across[None, : rows // 2], across[None, rows // 2 :]
    for step_x, step_y in ((1, 4), (3, 12), (4, 1)):
        by_x = jnp.concatenate([by_x, swap_tensor(by_x, step_x)], axis=0)
        by_y = jnp.concatenate([by_y, swap_tensor(by_y, step_y)], axis=0)
        by_x, by_y = lax.optimization_barrier((by_x, by_y))
    by_x, by_y, other_weight = lax.optimization_barrier((by_x, by_y, other_weight))
    swapped = [swap_core(by_x), swap_core(by_y)]
    late = [swap_tensor(by_x, 12), swap_tensor(by_y, 3)]
    ref_both, swapped, late = lax.optimization_barrier((ref_both, swapped, late))
    refer = lax.all_to_all(
        ref_both,
        ("dp", "tensor"),
        split_axis=0,
        concat_axis=0,
        tiled=True,
        axis_index_groups=[
            [(ring * CORES + c) * CHIPS + chip for ring in range(RING) for chip in range(CHIPS)] for c in range(CORES)
        ],
    )
    near, late = lax.optimization_barrier((near, late))
    near += [swap_core(a) for a in near]
    swapped += [swap_core(a) for a in late]
    gathered = [by_x, late[0], by_y, late[1], swapped[0], swapped[2], swapped[1], swapped[3]]
    policy = policy_logits(hidden, theirs, near, gathered, weight)
    refer, policy = lax.optimization_barrier((refer, policy))
    refer = refer.reshape(policy.shape)
    stats = row_stats(targets, policy, refer)

    for send, steps in (
        (swap_tensor, (1, 2, 3)),
        (swap_tensor, (4, 8, 12)),
        (swap_z, (1, 2, 3)),
    ):
        stats = merge([stats] + [send(stats, o) for o in steps])
    stats = merge([stats, swap_core(stats)])

    grad, loss = logit_grads(stats, targets, sequence, response, policy, refer, 2 * RING * CORES)

    sums = {4: [], 1: []}
    products = hidden_parts(grad, swap_core(grad), weight, other_weight)
    for part, (along_x, first) in enumerate(PARTS):
        send, keep = products[2 * part], products[2 * part + 1]
        axis = RING if along_x else 1
        got = swap_tensor(send, axis * first)
        n = keep.shape[0] // 2
        more = swap_tensor(add(keep[n:], got[n:]).astype(BF16), axis * (RING - first))
        sums[axis].append(add(keep[:n], got[:n], more).astype(BF16))
    ends = []
    for axis, cross in ((4, 1), (1, 4)):
        block = jnp.concatenate(sums[axis], axis=1)
        block = block.reshape(RING, block.shape[0] // RING, -1)
        ends.append(add(block[0], *[swap_tensor(block[k], cross * k) for k in (2, 1, 3)]).astype(BF16))
    ends = jnp.concatenate(ends, axis=1).reshape(RING, CORES * RING, half)
    d_half = add(ends[0], *[swap_z(ends[k], k) for k in (2, 1, 3)]).astype(BF16).reshape(CORES, RING, half)
    own_rows = lax.dynamic_index_in_dim(d_half, core, 0, keepdims=False)
    got_rows = swap_core(lax.dynamic_index_in_dim(d_half, 1 - core, 0, keepdims=False))
    d_hidden = jnp.where(
        core == 0, jnp.concatenate([own_rows, got_rows], axis=1), jnp.concatenate([got_rows, own_rows], axis=1)
    )
    return d_hidden, loss[0, 0]


def solution(mesh):
    in_specs = (P("dp", None), P(None, ("dp", "tensor")), P(("dp", "tensor"), None), P(), P(), P())
    out_specs = (P(("dp", "tensor"), None), P())
    return jax.shard_map(shards, mesh=mesh, in_specs=in_specs, out_specs=out_specs, check_vma=False)
```

```python
import functools

import jax
import jax.numpy as jnp
from jax import lax
from jax.experimental import pallas as pl
from jax.experimental.pallas import tpu as pltpu
from jax.sharding import PartitionSpec as P

BETA = 0.05
KL_WEIGHT = 0.1
LOSS_SCALE = 1024.0
BF16 = jnp.bfloat16
F32 = jnp.float32

RING = 4
CORES = 2
CHIPS = RING * RING


def swap_tensor(value, offset):
    return lax.ppermute(value, "tensor", [(i, i ^ offset) for i in range(CHIPS)])


def swap_z(value, offset):
    return lax.ppermute(value, "dp", [(i, i ^ (offset * CORES)) for i in range(RING * CORES)])


def swap_core(value):
    return lax.ppermute(value, "dp", [(i, i ^ 1) for i in range(RING * CORES)])


def any_spec():
    return pl.BlockSpec(memory_space=pl.ANY)


def params(mib):
    return pltpu.CompilerParams(vmem_limit_bytes=mib * 1024 * 1024)


def place_of(first, second):
    b, e = first >> 1, second >> 1
    return ((first & 1) ^ b) + 2 * b + 4 * ((second & 1) ^ e) + 8 * e


def where_am_i():
    dp, t = lax.axis_index("dp"), lax.axis_index("tensor")
    return dp & 1, t >> 2, t & 3, dp >> 1


def logits_body(*refs):
    (mine, theirs), near, gathered, weight, policy_ref = refs[:2], refs[2:6], refs[6:14], refs[14], refs[15]
    states, pieces, slabs, sems = refs[16:]
    rows, width = mine.shape
    depth = width // (2 * RING)
    span = width // CHIPS
    core, x, y, z = where_am_i()

    def rows_of(dz, side, start=0, size=rows):
        start = (z ^ dz) * (2 * rows) + (core ^ side) * rows + start
        return pl.ds(pl.multiple_of(start, size), size)

    loads = [
        pltpu.make_async_copy(ref, pieces.at[i // 2, pl.ds(8 * (i % 2), 8)], sems.at[i]) for i, ref in enumerate(gathered)
    ]
    blocks = [(0, 0, mine), (0, 1, theirs), (1, 0, near[0]), (3, 0, near[1]), (1, 1, near[2]), (3, 1, near[3])]
    slices = []
    for k in range(2 * RING):
        here = pl.ds(k * depth, depth)
        moves = [(block.at[:, here], states.at[rows_of(dz, side), here]) for dz, side, block in blocks]
        moves.append((weight.at[here], slabs.at[k]))
        slices.append([pltpu.make_async_copy(a, b, sems.at[8 + 7 * k + i]) for i, (a, b) in enumerate(moves)])
    for copy in loads + slices[0]:
        copy.start()
    for k in range(1, 2 * RING):
        for copy in slices[k]:
            copy.start()
    for copy in loads:
        copy.wait()
    for i in range(CHIPS):
        dx, dy = x ^ (i // RING), y ^ (i % RING)
        at = pl.ds(i * span, span)
        for side in range(CORES):
            states[rows_of(2, side, 0, rows // 2), at] = pieces[2 * side, place_of(dy, dx)]
            states[rows_of(2, side, rows // 2, rows // 2), at] = pieces[2 * side + 1, place_of(dx, dy)]
    for k in range(2 * RING):
        for copy in slices[k]:
            copy.wait()
        product = jnp.dot(states[:, k * depth : (k + 1) * depth], slabs[k], preferred_element_type=F32)
        policy_ref[...] = product if k == 0 else policy_ref[...] + product


def policy_logits(mine, theirs, near, gathered, weight):
    rows, width = mine.shape
    tokens = rows * CORES * RING
    cols = weight.shape[1]
    return pl.pallas_call(
        logits_body,
        out_shape=jax.ShapeDtypeStruct((tokens, cols), F32),
        in_specs=[any_spec()] * 15,
        out_specs=pl.BlockSpec(memory_space=pltpu.VMEM),
        scratch_shapes=[
            pltpu.VMEM((tokens, width), BF16),
            pltpu.VMEM((4, CHIPS, rows // 2, width // CHIPS), BF16),
            pltpu.VMEM((2 * RING, width // (2 * RING), cols), BF16),
            pltpu.SemaphoreType.DMA((8 + 7 * 2 * RING,)),
        ],
        compiler_params=params(52),
        cost_estimate=pl.CostEstimate(flops=tokens * cols, bytes_accessed=tokens * cols, transcendentals=0),
        name="policy_logits",
    )(mine, theirs, *near, *gathered, weight)


def in_token_order(refer, own):
    shape = (refer.shape[0], refer.shape[0])
    row, source = lax.broadcasted_iota(jnp.int32, shape, 0), lax.broadcasted_iota(jnp.int32, shape, 1)
    wanted = ((row >> 2) & 15) * 8 + ((row >> 6) ^ own) * 4 + (row & 3)
    return jnp.dot((source == wanted).astype(F32).astype(BF16), refer, preferred_element_type=F32)


def stats_body(targets_ref, policy_ref, refer_ref, stats_ref):
    rows, cols = policy_ref.shape
    core, x, y, z = where_am_i()
    start_col = (((z * CORES + core) * RING + x) * RING + y) * cols
    local = targets_ref[...].reshape(1, rows) - start_col
    local = jnp.where((local >= 0) & (local < cols), local, -1).astype(F32)
    local = jnp.broadcast_to(local, (128, rows)).T[:, 0:1].astype(jnp.int32)
    stats_ref[...] = block_stats(local, policy_ref[...], in_token_order(refer_ref[...], core))


def block_stats(local, policy, refer):
    rows, cols = policy.shape
    hit = lax.broadcasted_iota(jnp.int32, (rows, cols), 1) == local
    peak = jnp.max(policy, axis=1, keepdims=True)
    scaled = jnp.exp(policy - peak)
    total = jnp.sum(scaled, axis=1, keepdims=True)
    cross = jnp.sum(scaled * (policy - refer), axis=1, keepdims=True)
    ref_peak = jnp.max(refer, axis=1, keepdims=True)
    ref_total = jnp.sum(jnp.exp(refer - ref_peak), axis=1, keepdims=True)
    picked = jnp.sum(jnp.where(hit, policy, 0.0), axis=1, keepdims=True)
    ref_picked = jnp.sum(jnp.where(hit, refer, 0.0), axis=1, keepdims=True)
    lane = lax.broadcasted_iota(jnp.int32, (rows, 128), 1)
    table = jnp.zeros((rows, 128), F32)
    for k, value in enumerate((peak, total, cross, ref_peak, ref_total, picked, ref_picked)):
        table = jnp.where(lane == k, value, table)
    return table.T[:8]


def row_stats(targets, policy, refer):
    tokens, cols = policy.shape
    step = 128
    return pl.pallas_call(
        stats_body,
        grid=(tokens // step,),
        out_shape=jax.ShapeDtypeStruct((8, tokens), F32),
        in_specs=[
            pl.BlockSpec((step,), lambda i: (i,)),
            pl.BlockSpec((step, cols), lambda i: (i, 0)),
            pl.BlockSpec((step, cols), lambda i: (i, 0)),
        ],
        out_specs=pl.BlockSpec((8, step), lambda i: (0, i)),
        compiler_params=params(24),
        cost_estimate=pl.CostEstimate(flops=20 * tokens * cols, bytes_accessed=6 * tokens * cols, transcendentals=2 * tokens * cols),
        name="row_stats",
    )(targets, policy, refer)


def merge(stats):
    table = jnp.stack(stats)
    peak = jnp.max(table[:, 0], axis=0)
    share = jnp.exp(table[:, 0] - peak)
    total = jnp.sum(share * table[:, 1], axis=0)
    cross = jnp.sum(share * table[:, 2], axis=0)
    ref_peak = jnp.max(table[:, 3], axis=0)
    ref_total = jnp.sum(jnp.exp(table[:, 3] - ref_peak) * table[:, 4], axis=0)
    picked = jnp.sum(table[:, 5], axis=0)
    ref_picked = jnp.sum(table[:, 6], axis=0)
    return jnp.stack([peak, total, cross, ref_peak, ref_total, picked, ref_picked, jnp.zeros_like(peak)])


def grad_body(n_seq, stats_ref, targets_ref, sequence_ref, response_ref, policy_ref, refer_ref, grad_ref, loss_ref):
    tokens, cols = policy_ref.shape
    core_here, x, y, z = where_am_i()
    start_col = (((z * CORES + core_here) * RING + x) * RING + y) * cols
    stats = stats_ref[...]
    peak, total, cross, ref_peak, ref_total, picked, ref_picked = [stats[k : k + 1] for k in range(7)]
    targets, sequence, response = [ref[...].reshape(1, tokens) for ref in (targets_ref, sequence_ref, response_ref)]
    log_total = peak + jnp.log(total)
    ref_log_total = ref_peak + jnp.log(ref_total)
    mean_gap = cross / total
    diverge = mean_gap - log_total + ref_log_total
    mask = response.astype(F32)
    delta = mask * ((picked - log_total) - (ref_picked - ref_log_total))
    ids = lax.broadcasted_iota(jnp.int32, (n_seq, tokens), 0)
    member = (ids == sequence).astype(F32)
    pair = lax.broadcasted_iota(jnp.int32, (n_seq // 2, tokens), 0)
    side = jnp.where(pair == sequence >> 1, jnp.where((sequence & 1) == 0, 1.0, -1.0), 0.0)
    margin = BETA * jnp.sum(side * delta, axis=1, keepdims=True)
    pull = BETA * jax.nn.sigmoid(-margin)
    token_grad = -jnp.sum(side * pull, axis=0, keepdims=True)
    losses = jnp.maximum(-margin, 0.0) + jnp.log1p(jnp.exp(-jnp.abs(margin)))
    objective = jnp.sum(losses) + KL_WEIGHT * jnp.sum(mask * diverge)
    loss_ref[...] = jnp.full(loss_ref.shape, objective / tokens, F32)

    lift = LOSS_SCALE * mask
    local = targets - start_col
    local = jnp.where((local >= 0) & (local < cols), local, -1).astype(F32)
    rows8 = lax.broadcasted_iota(jnp.int32, (128, tokens), 0)
    packed = jnp.zeros((128, tokens), F32)
    for k, value in enumerate((log_total, mean_gap, lift * token_grad, lift * KL_WEIGHT, local)):
        packed = jnp.where(rows8 == k, value, packed)
    packed = packed.T

    step = 128
    pieces = []
    for i in range(tokens // step):
        span = slice(i * step, (i + 1) * step)
        per_row = packed[span]
        policy = policy_ref[span, :]
        refer = in_token_order(refer_ref[span, :], core_here)
        column = lax.broadcasted_iota(jnp.int32, (step, cols), 1)
        hit = (column == per_row[:, 4:5].astype(jnp.int32)).astype(F32)
        probs = jnp.exp(policy - per_row[:, 0:1])
        grad = per_row[:, 2:3] * (hit - probs) + per_row[:, 3:4] * probs * ((policy - refer) - per_row[:, 1:2])
        pieces.append(grad.astype(BF16))
    grad = jnp.concatenate(pieces, axis=0)

    row = lax.broadcasted_iota(jnp.int32, (tokens, tokens), 0)
    token = lax.broadcasted_iota(jnp.int32, (tokens, tokens), 1)
    dx, dy, dz, core, t = row >> 7, (row >> 5) & 3, (row >> 3) & 3, (row >> 2) & 1, row & 3
    source = (z ^ dz) * 128 + core * 64 + (x ^ dx) * 16 + (y ^ dy) * 4 + t
    pick = (token == source).astype(F32).astype(BF16)
    grad_ref[...] = jnp.dot(pick, grad, preferred_element_type=F32).astype(BF16)


def logit_grads(stats, targets, sequence, response, policy, refer, n_seq):
    tokens, cols = policy.shape
    vmem = pl.BlockSpec(memory_space=pltpu.VMEM)
    return pl.pallas_call(
        functools.partial(grad_body, n_seq),
        out_shape=(
            jax.ShapeDtypeStruct((tokens, cols), BF16),
            jax.ShapeDtypeStruct((8, 128), F32),
        ),
        in_specs=[vmem] * 6,
        out_specs=(vmem, vmem),
        compiler_params=params(24),
        cost_estimate=pl.CostEstimate(flops=2 * tokens * tokens * cols, bytes_accessed=10 * tokens * cols, transcendentals=tokens * cols),
        name="logit_grads",
    )(stats, targets, sequence, response, policy, refer)


PARTS = ((True, 1), (True, 3), (False, 1), (False, 3))
SENDS = {1: (1, 2), 3: (3, 2)}
KEEPS = {1: (0, 3), 3: (0, 1)}


def hidden_body(own_grad, other_grad, own_weight, other_weight, *refs):
    outs, (grads, slabs, results, sems) = refs[:8], refs[8:]
    tokens, cols = own_grad.shape
    core = lax.axis_index("dp") & 1
    half = own_weight.shape[0] // CORES
    depth = half // 4
    step = depth // 2
    loads = [
        pltpu.make_async_copy(ref, grads.at[:, pl.ds(i * cols, cols)], sems.at[i])
        for i, ref in enumerate((own_grad, other_grad))
    ]
    fetches = []
    for i in range(8):
        rows = pl.ds(pl.multiple_of(core * half + i * step, step), step)
        fetches.append(
            [
                pltpu.make_async_copy(ref.at[rows], slabs.at[i, :, pl.ds(n * cols, cols)], sems.at[2 + 2 * i + n])
                for n, ref in enumerate((own_weight, other_weight))
            ]
        )
    stores = [pltpu.make_async_copy(results.at[i], outs[i], sems.at[18 + i]) for i in range(8)]
    for copy in loads + sum(fetches, []):
        copy.start()
    for copy in loads:
        copy.wait()
    unit = tokens // CHIPS
    for i in range(8):
        part = i // 2
        along_x, first = PARTS[part]
        for copy in fetches[i]:
            copy.wait()
        product = lax.dot_general(grads[...], slabs[i], (((1,), (1,)), ((), ())), preferred_element_type=F32).astype(BF16)
        for n, order in ((2 * part, SENDS[first]), (2 * part + 1, KEEPS[first])):
            for k, outer in enumerate(order):
                for inner in range(RING):
                    source = (outer * RING + inner) if along_x else (inner * RING + outer)
                    there = (k * RING + inner) * unit
                    results[n, there : there + unit, (i % 2) * step : (i % 2 + 1) * step] = product[
                        source * unit : (source + 1) * unit
                    ]
        if i % 2 == 1:
            stores[2 * part].start()
            stores[2 * part + 1].start()
    for copy in stores:
        copy.wait()


def hidden_parts(own_grad, other_grad, weight, other_weight):
    tokens, cols = own_grad.shape
    depth = weight.shape[0] // CORES // 4
    return pl.pallas_call(
        hidden_body,
        out_shape=(jax.ShapeDtypeStruct((tokens // 2, depth), BF16),) * 8,
        in_specs=[any_spec()] * 4,
        out_specs=(any_spec(),) * 8,
        scratch_shapes=[
            pltpu.VMEM((tokens, CORES * cols), BF16),
            pltpu.VMEM((8, depth // 2, CORES * cols), BF16),
            pltpu.VMEM((8, tokens // 2, depth), BF16),
            pltpu.SemaphoreType.DMA((26,)),
        ],
        compiler_params=params(50),
        cost_estimate=pl.CostEstimate(
            flops=16 * tokens * depth * cols, bytes_accessed=16 * cols * (tokens + depth) + 8 * tokens * depth, transcendentals=0
        ),
        name="hidden_parts",
    )(own_grad, other_grad, weight, other_weight)


def add(*terms):
    total = terms[0].astype(F32)
    for term in terms[1:]:
        total = total + term.astype(F32)
    return total


def shards(hidden, weight, ref_logits, targets, sequence, response):
    rows, width = hidden.shape
    cols = weight.shape[1]
    half = width // CORES
    dp, t = lax.axis_index("dp"), lax.axis_index("tensor")
    z, core = dp // CORES, dp % CORES
    x, y = t // RING, t % RING

    piece = width // CHIPS
    across = [
        lax.dynamic_slice(hidden, (first, (t ^ offset) * piece), (rows // 2, piece))
        for first, offset in ((0, 0), (0, 1), (rows // 2, 0), (rows // 2, RING))
    ]
    across = swap_z(jnp.stack(across), 2)
    sent, across = lax.optimization_barrier((hidden, across))
    near = [swap_z(sent, 1), swap_z(sent, 3)]
    other_weight = swap_core(weight)
    theirs = swap_core(hidden)
    ref_logits = ref_logits.reshape(RING, RING, CORES, CHIPS, cols)
    ref_own, ref_other = [
        lax.dynamic_index_in_dim(ref_logits, c, 2, keepdims=False).transpose(1, 2, 0, 3).reshape(RING * CHIPS, RING, cols)
        for c in (core, 1 - core)
    ]
    ref_other = swap_core(ref_other)
    ref_both = jnp.concatenate([ref_own, ref_other], axis=1)
    by_x, by_y = across[:2], across[2:]
    for step_x, step_y in ((3, 12), (4, 1)):
        by_x = jnp.concatenate([by_x, swap_tensor(by_x, step_x)], axis=0)
        by_y = jnp.concatenate([by_y, swap_tensor(by_y, step_y)], axis=0)
        by_x, by_y = lax.optimization_barrier((by_x, by_y))
    by_x, by_y, other_weight = lax.optimization_barrier((by_x, by_y, other_weight))
    swapped = [swap_core(by_x), swap_core(by_y)]
    late = [swap_tensor(by_x, 12), swap_tensor(by_y, 3)]
    near, late = lax.optimization_barrier((near, late))
    near += [swap_core(a) for a in near]
    swapped += [swap_core(a) for a in late]
    ref_both, near, swapped = lax.optimization_barrier((ref_both, near, swapped))
    refer = lax.all_to_all(
        ref_both,
        ("dp", "tensor"),
        split_axis=0,
        concat_axis=0,
        tiled=True,
        axis_index_groups=[
            [(ring * CORES + c) * CHIPS + chip for ring in range(RING) for chip in range(CHIPS)] for c in range(CORES)
        ],
    )
    gathered = [by_x, late[0], by_y, late[1], swapped[0], swapped[2], swapped[1], swapped[3]]
    policy = policy_logits(hidden, theirs, near, gathered, weight)
    refer, policy = lax.optimization_barrier((refer, policy))
    refer = refer.reshape(policy.shape)
    stats = row_stats(targets, policy, refer)

    for send, steps in (
        (swap_tensor, (1, 2, 3)),
        (swap_tensor, (4, 8, 12)),
        (swap_z, (1, 2, 3)),
    ):
        stats = merge([stats] + [send(stats, o) for o in steps])
    stats = merge([stats, swap_core(stats)])

    grad, loss = logit_grads(stats, targets, sequence, response, policy, refer, 2 * RING * CORES)

    sums = {4: [], 1: []}
    products = hidden_parts(grad, swap_core(grad), weight, other_weight)
    for part, (along_x, first) in enumerate(PARTS):
        send, keep = products[2 * part], products[2 * part + 1]
        axis = RING if along_x else 1
        got = swap_tensor(send, axis * first)
        n = keep.shape[0] // 2
        more = swap_tensor(add(keep[n:], got[n:]).astype(BF16), axis * (RING - first))
        sums[axis].append(add(keep[:n], got[:n], more).astype(BF16))
    ends = []
    for axis, cross in ((4, 1), (1, 4)):
        block = jnp.concatenate(sums[axis], axis=1)
        block = block.reshape(RING, block.shape[0] // RING, -1)
        ends.append(add(block[0], *[swap_tensor(block[k], cross * k) for k in (2, 1, 3)]).astype(BF16))
    ends = jnp.concatenate(ends, axis=1).reshape(RING, CORES * RING, half)
    d_half = add(ends[0], *[swap_z(ends[k], k) for k in (2, 1, 3)]).astype(BF16).reshape(CORES, RING, half)
    own_rows = lax.dynamic_index_in_dim(d_half, core, 0, keepdims=False)
    got_rows = swap_core(lax.dynamic_index_in_dim(d_half, 1 - core, 0, keepdims=False))
    d_hidden = jnp.where(
        core == 0, jnp.concatenate([own_rows, got_rows], axis=1), jnp.concatenate([got_rows, own_rows], axis=1)
    )
    return d_hidden, loss[0, 0]


def solution(mesh):
    in_specs = (P("dp", None), P(None, ("dp", "tensor")), P(("dp", "tensor"), None), P(), P(), P())
    out_specs = (P(("dp", "tensor"), None), P())
    return jax.shard_map(shards, mesh=mesh, in_specs=in_specs, out_specs=out_specs, check_vma=False)
```

```python
import functools

import jax
import jax.numpy as jnp
from jax import lax
from jax.experimental import pallas as pl
from jax.experimental.pallas import tpu as pltpu
from jax.sharding import PartitionSpec as P

BETA = 0.05
KL_WEIGHT = 0.1
LOSS_SCALE = 1024.0
BF16 = jnp.bfloat16
F32 = jnp.float32

RING = 4
CORES = 2
CHIPS = RING * RING


def swap_tensor(value, offset):
    return lax.ppermute(value, "tensor", [(i, i ^ offset) for i in range(CHIPS)])


def swap_z(value, offset):
    return lax.ppermute(value, "dp", [(i, i ^ (offset * CORES)) for i in range(RING * CORES)])


def swap_core(value):
    return lax.ppermute(value, "dp", [(i, i ^ 1) for i in range(RING * CORES)])


def any_spec():
    return pl.BlockSpec(memory_space=pl.ANY)


def params(mib):
    return pltpu.CompilerParams(vmem_limit_bytes=mib * 1024 * 1024)


def place_of(first, second):
    b, e = first >> 1, second >> 1
    return ((first & 1) ^ b) + 2 * b + 4 * ((second & 1) ^ e) + 8 * e


def where_am_i():
    dp, t = lax.axis_index("dp"), lax.axis_index("tensor")
    return dp & 1, t >> 2, t & 3, dp >> 1


def logits_body(*refs):
    (mine, theirs), near, gathered, weight, policy_ref = refs[:2], refs[2:6], refs[6:10], refs[10], refs[11]
    states, pieces, slabs, sems = refs[12:]
    rows, width = mine.shape
    depth = width // (2 * RING)
    span = width // CHIPS
    core, x, y, z = where_am_i()

    def rows_of(dz, side, start=0, size=rows):
        start = (z ^ dz) * (2 * rows) + (core ^ side) * rows + start
        return pl.ds(pl.multiple_of(start, size), size)

    loads = [
        pltpu.make_async_copy(ref, pieces.at[i], sems.at[i]) for i, ref in enumerate(gathered)
    ]
    blocks = [(0, 0, mine), (0, 1, theirs), (1, 0, near[0]), (3, 0, near[1]), (1, 1, near[2]), (3, 1, near[3])]
    slices = []
    for k in range(2 * RING):
        here = pl.ds(k * depth, depth)
        moves = [(block.at[:, here], states.at[rows_of(dz, side), here]) for dz, side, block in blocks]
        moves.append((weight.at[here], slabs.at[k]))
        slices.append([pltpu.make_async_copy(a, b, sems.at[8 + 7 * k + i]) for i, (a, b) in enumerate(moves)])
    for copy in loads + slices[0]:
        copy.start()
    for k in range(1, 2 * RING):
        for copy in slices[k]:
            copy.start()
    for copy in loads:
        copy.wait()
    for i in range(CHIPS):
        dx, dy = x ^ (i // RING), y ^ (i % RING)
        at = pl.ds(i * span, span)
        for side in range(CORES):
            states[rows_of(2, side, 0, rows // 2), at] = pieces[2 * side, place_of(dy, dx)]
            states[rows_of(2, side, rows // 2, rows // 2), at] = pieces[2 * side + 1, place_of(dx, dy)]
    for k in range(2 * RING):
        for copy in slices[k]:
            copy.wait()
        product = jnp.dot(states[:, k * depth : (k + 1) * depth], slabs[k], preferred_element_type=F32)
        policy_ref[...] = product if k == 0 else policy_ref[...] + product


def policy_logits(mine, theirs, near, gathered, weight):
    rows, width = mine.shape
    tokens = rows * CORES * RING
    cols = weight.shape[1]
    return pl.pallas_call(
        logits_body,
        out_shape=jax.ShapeDtypeStruct((tokens, cols), F32),
        in_specs=[any_spec()] * 11,
        out_specs=pl.BlockSpec(memory_space=pltpu.VMEM),
        scratch_shapes=[
            pltpu.VMEM((tokens, width), BF16),
            pltpu.VMEM((4, CHIPS, rows // 2, width // CHIPS), BF16),
            pltpu.VMEM((2 * RING, width // (2 * RING), cols), BF16),
            pltpu.SemaphoreType.DMA((8 + 7 * 2 * RING,)),
        ],
        compiler_params=params(52),
        cost_estimate=pl.CostEstimate(flops=tokens * cols, bytes_accessed=tokens * cols, transcendentals=0),
        name="policy_logits",
    )(mine, theirs, *near, *gathered, weight)


def in_token_order(refer, own):
    shape = (refer.shape[0], refer.shape[0])
    row, source = lax.broadcasted_iota(jnp.int32, shape, 0), lax.broadcasted_iota(jnp.int32, shape, 1)
    wanted = ((row >> 2) & 15) * 8 + ((row >> 6) ^ own) * 4 + (row & 3)
    return jnp.dot((source == wanted).astype(F32).astype(BF16), refer, preferred_element_type=F32)


def stats_body(targets_ref, policy_ref, refer_ref, stats_ref):
    rows, cols = policy_ref.shape
    core, x, y, z = where_am_i()
    start_col = (((z * CORES + core) * RING + x) * RING + y) * cols
    local = targets_ref[...].reshape(1, rows) - start_col
    local = jnp.where((local >= 0) & (local < cols), local, -1).astype(F32)
    local = jnp.broadcast_to(local, (128, rows)).T[:, 0:1].astype(jnp.int32)
    stats_ref[...] = block_stats(local, policy_ref[...], in_token_order(refer_ref[...], core))


def block_stats(local, policy, refer):
    rows, cols = policy.shape
    hit = lax.broadcasted_iota(jnp.int32, (rows, cols), 1) == local
    peak = jnp.max(policy, axis=1, keepdims=True)
    scaled = jnp.exp(policy - peak)
    total = jnp.sum(scaled, axis=1, keepdims=True)
    cross = jnp.sum(scaled * (policy - refer), axis=1, keepdims=True)
    ref_peak = jnp.max(refer, axis=1, keepdims=True)
    ref_total = jnp.sum(jnp.exp(refer - ref_peak), axis=1, keepdims=True)
    picked = jnp.sum(jnp.where(hit, policy, 0.0), axis=1, keepdims=True)
    ref_picked = jnp.sum(jnp.where(hit, refer, 0.0), axis=1, keepdims=True)
    lane = lax.broadcasted_iota(jnp.int32, (rows, 128), 1)
    table = jnp.zeros((rows, 128), F32)
    for k, value in enumerate((peak, total, cross, ref_peak, ref_total, picked, ref_picked)):
        table = jnp.where(lane == k, value, table)
    return table.T[:8]


def row_stats(targets, policy, refer):
    tokens, cols = policy.shape
    step = 128
    return pl.pallas_call(
        stats_body,
        grid=(tokens // step,),
        out_shape=jax.ShapeDtypeStruct((8, tokens), F32),
        in_specs=[
            pl.BlockSpec((step,), lambda i: (i,)),
            pl.BlockSpec((step, cols), lambda i: (i, 0)),
            pl.BlockSpec((step, cols), lambda i: (i, 0)),
        ],
        out_specs=pl.BlockSpec((8, step), lambda i: (0, i)),
        compiler_params=params(24),
        cost_estimate=pl.CostEstimate(flops=20 * tokens * cols, bytes_accessed=6 * tokens * cols, transcendentals=2 * tokens * cols),
        name="row_stats",
    )(targets, policy, refer)


def merge(stats):
    table = jnp.stack(stats)
    peak = jnp.max(table[:, 0], axis=0)
    share = jnp.exp(table[:, 0] - peak)
    total = jnp.sum(share * table[:, 1], axis=0)
    cross = jnp.sum(share * table[:, 2], axis=0)
    ref_peak = jnp.max(table[:, 3], axis=0)
    ref_total = jnp.sum(jnp.exp(table[:, 3] - ref_peak) * table[:, 4], axis=0)
    picked = jnp.sum(table[:, 5], axis=0)
    ref_picked = jnp.sum(table[:, 6], axis=0)
    return jnp.stack([peak, total, cross, ref_peak, ref_total, picked, ref_picked, jnp.zeros_like(peak)])


def grad_body(n_seq, stats_ref, targets_ref, sequence_ref, response_ref, policy_ref, refer_ref, grad_ref, loss_ref):
    tokens, cols = policy_ref.shape
    core_here, x, y, z = where_am_i()
    start_col = (((z * CORES + core_here) * RING + x) * RING + y) * cols
    stats = stats_ref[...]
    peak, total, cross, ref_peak, ref_total, picked, ref_picked = [stats[k : k + 1] for k in range(7)]
    targets, sequence, response = [ref[...].reshape(1, tokens) for ref in (targets_ref, sequence_ref, response_ref)]
    log_total = peak + jnp.log(total)
    ref_log_total = ref_peak + jnp.log(ref_total)
    mean_gap = cross / total
    diverge = mean_gap - log_total + ref_log_total
    mask = response.astype(F32)
    delta = mask * ((picked - log_total) - (ref_picked - ref_log_total))
    ids = lax.broadcasted_iota(jnp.int32, (n_seq, tokens), 0)
    member = (ids == sequence).astype(F32)
    pair = lax.broadcasted_iota(jnp.int32, (n_seq // 2, tokens), 0)
    side = jnp.where(pair == sequence >> 1, jnp.where((sequence & 1) == 0, 1.0, -1.0), 0.0)
    margin = BETA * jnp.sum(side * delta, axis=1, keepdims=True)
    pull = BETA * jax.nn.sigmoid(-margin)
    token_grad = -jnp.sum(side * pull, axis=0, keepdims=True)
    losses = jnp.maximum(-margin, 0.0) + jnp.log1p(jnp.exp(-jnp.abs(margin)))
    objective = jnp.sum(losses) + KL_WEIGHT * jnp.sum(mask * diverge)
    loss_ref[...] = jnp.full(loss_ref.shape, objective / tokens, F32)

    lift = LOSS_SCALE * mask
    local = targets - start_col
    local = jnp.where((local >= 0) & (local < cols), local, -1).astype(F32)
    rows8 = lax.broadcasted_iota(jnp.int32, (128, tokens), 0)
    packed = jnp.zeros((128, tokens), F32)
    for k, value in enumerate((log_total, mean_gap, lift * token_grad, lift * KL_WEIGHT, local)):
        packed = jnp.where(rows8 == k, value, packed)
    packed = packed.T

    step = 128
    pieces = []
    for i in range(tokens // step):
        span = slice(i * step, (i + 1) * step)
        per_row = packed[span]
        policy = policy_ref[span, :]
        refer = in_token_order(refer_ref[span, :], core_here)
        column = lax.broadcasted_iota(jnp.int32, (step, cols), 1)
        hit = (column == per_row[:, 4:5].astype(jnp.int32)).astype(F32)
        probs = jnp.exp(policy - per_row[:, 0:1])
        grad = per_row[:, 2:3] * (hit - probs) + per_row[:, 3:4] * probs * ((policy - refer) - per_row[:, 1:2])
        pieces.append(grad.astype(BF16))
    grad = jnp.concatenate(pieces, axis=0)

    row = lax.broadcasted_iota(jnp.int32, (tokens, tokens), 0)
    token = lax.broadcasted_iota(jnp.int32, (tokens, tokens), 1)
    dx, dy, dz, core, t = row >> 7, (row >> 5) & 3, (row >> 3) & 3, (row >> 2) & 1, row & 3
    source = (z ^ dz) * 128 + core * 64 + (x ^ dx) * 16 + (y ^ dy) * 4 + t
    pick = (token == source).astype(F32).astype(BF16)
    grad_ref[...] = jnp.dot(pick, grad, preferred_element_type=F32).astype(BF16)


def logit_grads(stats, targets, sequence, response, policy, refer, n_seq):
    tokens, cols = policy.shape
    vmem = pl.BlockSpec(memory_space=pltpu.VMEM)
    return pl.pallas_call(
        functools.partial(grad_body, n_seq),
        out_shape=(
            jax.ShapeDtypeStruct((tokens, cols), BF16),
            jax.ShapeDtypeStruct((8, 128), F32),
        ),
        in_specs=[vmem] * 6,
        out_specs=(vmem, vmem),
        compiler_params=params(24),
        cost_estimate=pl.CostEstimate(flops=2 * tokens * tokens * cols, bytes_accessed=10 * tokens * cols, transcendentals=tokens * cols),
        name="logit_grads",
    )(stats, targets, sequence, response, policy, refer)


PARTS = ((True, 1), (True, 3), (False, 1), (False, 3))
SENDS = {1: (1, 2), 3: (3, 2)}
KEEPS = {1: (0, 3), 3: (0, 1)}


def hidden_body(own_grad, other_grad, own_weight, other_weight, *refs):
    outs, (grads, slabs, results, sems) = refs[:8], refs[8:]
    tokens, cols = own_grad.shape
    core = lax.axis_index("dp") & 1
    half = own_weight.shape[0] // CORES
    depth = half // 4
    step = depth // 2
    loads = [
        pltpu.make_async_copy(ref, grads.at[:, pl.ds(i * cols, cols)], sems.at[i])
        for i, ref in enumerate((own_grad, other_grad))
    ]
    fetches = []
    for i in range(8):
        rows = pl.ds(pl.multiple_of(core * half + i * step, step), step)
        fetches.append(
            [
                pltpu.make_async_copy(ref.at[rows], slabs.at[i, :, pl.ds(n * cols, cols)], sems.at[2 + 2 * i + n])
                for n, ref in enumerate((own_weight, other_weight))
            ]
        )
    stores = [pltpu.make_async_copy(results.at[i], outs[i], sems.at[18 + i]) for i in range(8)]
    for copy in loads + sum(fetches, []):
        copy.start()
    for copy in loads:
        copy.wait()
    unit = tokens // CHIPS
    for i in range(8):
        part = i // 2
        along_x, first = PARTS[part]
        for copy in fetches[i]:
            copy.wait()
        product = lax.dot_general(grads[...], slabs[i], (((1,), (1,)), ((), ())), preferred_element_type=F32).astype(BF16)
        for n, order in ((2 * part, SENDS[first]), (2 * part + 1, KEEPS[first])):
            for k, outer in enumerate(order):
                for inner in range(RING):
                    source = (outer * RING + inner) if along_x else (inner * RING + outer)
                    there = (k * RING + inner) * unit
                    results[n, there : there + unit, (i % 2) * step : (i % 2 + 1) * step] = product[
                        source * unit : (source + 1) * unit
                    ]
        if i % 2 == 1:
            stores[2 * part].start()
            stores[2 * part + 1].start()
    for copy in stores:
        copy.wait()


def hidden_parts(own_grad, other_grad, weight, other_weight):
    tokens, cols = own_grad.shape
    depth = weight.shape[0] // CORES // 4
    return pl.pallas_call(
        hidden_body,
        out_shape=(jax.ShapeDtypeStruct((tokens // 2, depth), BF16),) * 8,
        in_specs=[any_spec()] * 4,
        out_specs=(any_spec(),) * 8,
        scratch_shapes=[
            pltpu.VMEM((tokens, CORES * cols), BF16),
            pltpu.VMEM((8, depth // 2, CORES * cols), BF16),
            pltpu.VMEM((8, tokens // 2, depth), BF16),
            pltpu.SemaphoreType.DMA((26,)),
        ],
        compiler_params=params(50),
        cost_estimate=pl.CostEstimate(
            flops=16 * tokens * depth * cols, bytes_accessed=16 * cols * (tokens + depth) + 8 * tokens * depth, transcendentals=0
        ),
        name="hidden_parts",
    )(own_grad, other_grad, weight, other_weight)


def add(*terms):
    total = terms[0].astype(F32)
    for term in terms[1:]:
        total = total + term.astype(F32)
    return total


def shards(hidden, weight, ref_logits, targets, sequence, response):
    rows, width = hidden.shape
    cols = weight.shape[1]
    half = width // CORES
    dp, t = lax.axis_index("dp"), lax.axis_index("tensor")
    z, core = dp // CORES, dp % CORES
    x, y = t // RING, t % RING

    piece = width // CHIPS
    across = [
        lax.dynamic_slice(hidden, (first, (t ^ offset) * piece), (rows // 2, piece))
        for first, offset in ((0, 0), (0, 1), (rows // 2, 0), (rows // 2, RING))
    ]
    across = swap_z(jnp.stack(across), 2)
    sent, across = lax.optimization_barrier((hidden, across))
    near = [swap_z(sent, 1), swap_z(sent, 3)]
    other_weight = swap_core(weight)
    theirs = swap_core(hidden)
    ref_logits = ref_logits.reshape(RING, RING, CORES, CHIPS, cols)
    ref_own, ref_other = [
        lax.dynamic_index_in_dim(ref_logits, c, 2, keepdims=False).transpose(1, 2, 0, 3).reshape(RING * CHIPS, RING, cols)
        for c in (core, 1 - core)
    ]
    ref_other = swap_core(ref_other)
    ref_both = jnp.concatenate([ref_own, ref_other], axis=1)
    by_x, by_y = across[:2], across[2:]
    for step_x, step_y in ((3, 12), (4, 1)):
        by_x = jnp.concatenate([by_x, swap_tensor(by_x, step_x)], axis=0)
        by_y = jnp.concatenate([by_y, swap_tensor(by_y, step_y)], axis=0)
        by_x, by_y = lax.optimization_barrier((by_x, by_y))
    by_x, by_y, other_weight = lax.optimization_barrier((by_x, by_y, other_weight))
    late = [swap_tensor(by_x, 12), swap_tensor(by_y, 3)]
    ref_both, late = lax.optimization_barrier((ref_both, late))
    gathered = [jnp.concatenate(pair, axis=0) for pair in zip((by_x, by_y), late)]
    near, gathered = lax.optimization_barrier((near, gathered))
    near += [swap_core(a) for a in near]
    gathered += [swap_core(a) for a in gathered]
    ref_both, near, gathered = lax.optimization_barrier((ref_both, near, gathered))

    refer = lax.all_to_all(
        ref_both,
        ("dp", "tensor"),
        split_axis=0,
        concat_axis=0,
        tiled=True,
        axis_index_groups=[
            [(ring * CORES + c) * CHIPS + chip for ring in range(RING) for chip in range(CHIPS)] for c in range(CORES)
        ],
    )
    policy = policy_logits(hidden, theirs, near, gathered, weight)
    refer, policy = lax.optimization_barrier((refer, policy))
    refer = refer.reshape(policy.shape)
    stats = row_stats(targets, policy, refer)

    for send, steps in (
        (swap_tensor, (1, 2, 3)),
        (swap_tensor, (4, 8, 12)),
        (swap_z, (1, 2, 3)),
    ):
        stats = merge([stats] + [send(stats, o) for o in steps])
    stats = merge([stats, swap_core(stats)])

    grad, loss = logit_grads(stats, targets, sequence, response, policy, refer, 2 * RING * CORES)

    sums = {4: [], 1: []}
    products = hidden_parts(grad, swap_core(grad), weight, other_weight)
    for part, (along_x, first) in enumerate(PARTS):
        send, keep = products[2 * part], products[2 * part + 1]
        axis = RING if along_x else 1
        got = swap_tensor(send, axis * first)
        n = keep.shape[0] // 2
        more = swap_tensor(add(keep[n:], got[n:]).astype(BF16), axis * (RING - first))
        sums[axis].append(add(keep[:n], got[:n], more).astype(BF16))
    ends = []
    for axis, cross in ((4, 1), (1, 4)):
        block = jnp.concatenate(sums[axis], axis=1)
        block = block.reshape(RING, block.shape[0] // RING, -1)
        ends.append(add(block[0], *[swap_tensor(block[k], cross * k) for k in (2, 1, 3)]).astype(BF16))
    ends = jnp.concatenate(ends, axis=1).reshape(RING, CORES * RING, half)
    d_half = add(ends[0], *[swap_z(ends[k], k) for k in (2, 1, 3)]).astype(BF16).reshape(CORES, RING, half)
    own_rows = lax.dynamic_index_in_dim(d_half, core, 0, keepdims=False)
    got_rows = swap_core(lax.dynamic_index_in_dim(d_half, 1 - core, 0, keepdims=False))
    d_hidden = jnp.where(
        core == 0, jnp.concatenate([own_rows, got_rows], axis=1), jnp.concatenate([got_rows, own_rows], axis=1)
    )
    return d_hidden, loss[0, 0]


def solution(mesh):
    in_specs = (P("dp", None), P(None, ("dp", "tensor")), P(("dp", "tensor"), None), P(), P(), P())
    out_specs = (P(("dp", "tensor"), None), P())
    return jax.shard_map(shards, mesh=mesh, in_specs=in_specs, out_specs=out_specs, check_vma=False)
```

```python
import functools

import jax
import jax.numpy as jnp
from jax import lax
from jax.experimental import pallas as pl
from jax.experimental.pallas import tpu as pltpu
from jax.sharding import PartitionSpec as P

BETA = 0.05
KL_WEIGHT = 0.1
LOSS_SCALE = 1024.0
BF16 = jnp.bfloat16
F32 = jnp.float32

RING = 4
CORES = 2
CHIPS = RING * RING


def swap_tensor(value, offset):
    return lax.ppermute(value, "tensor", [(i, i ^ offset) for i in range(CHIPS)])


def swap_z(value, offset):
    return lax.ppermute(value, "dp", [(i, i ^ (offset * CORES)) for i in range(RING * CORES)])


def swap_core(value):
    return lax.ppermute(value, "dp", [(i, i ^ 1) for i in range(RING * CORES)])


def any_spec():
    return pl.BlockSpec(memory_space=pl.ANY)


def params(mib):
    return pltpu.CompilerParams(vmem_limit_bytes=mib * 1024 * 1024)


def place_of(first, second):
    b, e = first >> 1, second >> 1
    return ((first & 1) ^ b) + 2 * b + 4 * ((second & 1) ^ e) + 8 * e


def where_am_i():
    dp, t = lax.axis_index("dp"), lax.axis_index("tensor")
    return dp & 1, t >> 2, t & 3, dp >> 1


def logits_body(*refs):
    (mine, theirs), near, gathered, weight, policy_ref = refs[:2], refs[2:6], refs[6:14], refs[14], refs[15]
    states, pieces, slabs, sems = refs[16:]
    rows, width = mine.shape
    depth = width // (2 * RING)
    span = width // CHIPS
    core, x, y, z = where_am_i()

    def rows_of(dz, side, start=0, size=rows):
        start = (z ^ dz) * (2 * rows) + (core ^ side) * rows + start
        return pl.ds(pl.multiple_of(start, size), size)

    loads = [
        pltpu.make_async_copy(ref, pieces.at[i // 2, pl.ds(8 * (i % 2), 8)], sems.at[i]) for i, ref in enumerate(gathered)
    ]
    blocks = [(0, 0, mine), (0, 1, theirs), (1, 0, near[0]), (3, 0, near[1]), (1, 1, near[2]), (3, 1, near[3])]
    slices = []
    for k in range(2 * RING):
        here = pl.ds(k * depth, depth)
        moves = [(block.at[:, here], states.at[rows_of(dz, side), here]) for dz, side, block in blocks]
        moves.append((weight.at[here], slabs.at[k]))
        slices.append([pltpu.make_async_copy(a, b, sems.at[8 + 7 * k + i]) for i, (a, b) in enumerate(moves)])
    for copy in loads + slices[0]:
        copy.start()
    for k in range(1, 2 * RING):
        for copy in slices[k]:
            copy.start()
    for copy in loads:
        copy.wait()
    for i in range(CHIPS):
        dx, dy = x ^ (i // RING), y ^ (i % RING)
        at = pl.ds(i * span, span)
        for side in range(CORES):
            states[rows_of(2, side, 0, rows // 2), at] = pieces[2 * side, place_of(dy, dx)]
            states[rows_of(2, side, rows // 2, rows // 2), at] = pieces[2 * side + 1, place_of(dx, dy)]
    for k in range(2 * RING):
        for copy in slices[k]:
            copy.wait()
        product = jnp.dot(states[:, k * depth : (k + 1) * depth], slabs[k], preferred_element_type=F32)
        policy_ref[...] = product if k == 0 else policy_ref[...] + product


def policy_logits(mine, theirs, near, gathered, weight):
    rows, width = mine.shape
    tokens = rows * CORES * RING
    cols = weight.shape[1]
    return pl.pallas_call(
        logits_body,
        out_shape=jax.ShapeDtypeStruct((tokens, cols), F32),
        in_specs=[any_spec()] * 15,
        out_specs=pl.BlockSpec(memory_space=pltpu.VMEM),
        scratch_shapes=[
            pltpu.VMEM((tokens, width), BF16),
            pltpu.VMEM((4, CHIPS, rows // 2, width // CHIPS), BF16),
            pltpu.VMEM((2 * RING, width // (2 * RING), cols), BF16),
            pltpu.SemaphoreType.DMA((8 + 7 * 2 * RING,)),
        ],
        compiler_params=params(52),
        cost_estimate=pl.CostEstimate(flops=tokens * cols, bytes_accessed=tokens * cols, transcendentals=0),
        name="policy_logits",
    )(mine, theirs, *near, *gathered, weight)


def in_token_order(refer, own):
    shape = (refer.shape[0], refer.shape[0])
    row, source = lax.broadcasted_iota(jnp.int32, shape, 0), lax.broadcasted_iota(jnp.int32, shape, 1)
    wanted = ((row >> 2) & 15) * 8 + ((row >> 6) ^ own) * 4 + (row & 3)
    return jnp.dot((source == wanted).astype(F32).astype(BF16), refer, preferred_element_type=F32)


def stats_body(targets_ref, policy_ref, refer_ref, stats_ref):
    rows, cols = policy_ref.shape
    core, x, y, z = where_am_i()
    start_col = (((z * CORES + core) * RING + x) * RING + y) * cols
    local = targets_ref[...].reshape(1, rows) - start_col
    local = jnp.where((local >= 0) & (local < cols), local, -1).astype(F32)
    local = jnp.broadcast_to(local, (128, rows)).T[:, 0:1].astype(jnp.int32)
    stats_ref[...] = block_stats(local, policy_ref[...], in_token_order(refer_ref[...], core))


def block_stats(local, policy, refer):
    rows, cols = policy.shape
    hit = lax.broadcasted_iota(jnp.int32, (rows, cols), 1) == local
    peak = jnp.max(policy, axis=1, keepdims=True)
    scaled = jnp.exp(policy - peak)
    total = jnp.sum(scaled, axis=1, keepdims=True)
    cross = jnp.sum(scaled * (policy - refer), axis=1, keepdims=True)
    ref_peak = jnp.max(refer, axis=1, keepdims=True)
    ref_total = jnp.sum(jnp.exp(refer - ref_peak), axis=1, keepdims=True)
    picked = jnp.sum(jnp.where(hit, policy, 0.0), axis=1, keepdims=True)
    ref_picked = jnp.sum(jnp.where(hit, refer, 0.0), axis=1, keepdims=True)
    lane = lax.broadcasted_iota(jnp.int32, (rows, 128), 1)
    table = jnp.zeros((rows, 128), F32)
    for k, value in enumerate((peak, total, cross, ref_peak, ref_total, picked, ref_picked)):
        table = jnp.where(lane == k, value, table)
    return table.T[:8]


def row_stats(targets, policy, refer):
    tokens, cols = policy.shape
    step = 128
    return pl.pallas_call(
        stats_body,
        grid=(tokens // step,),
        out_shape=jax.ShapeDtypeStruct((8, tokens), F32),
        in_specs=[
            pl.BlockSpec((step,), lambda i: (i,)),
            pl.BlockSpec((step, cols), lambda i: (i, 0)),
            pl.BlockSpec((step, cols), lambda i: (i, 0)),
        ],
        out_specs=pl.BlockSpec((8, step), lambda i: (0, i)),
        compiler_params=params(24),
        cost_estimate=pl.CostEstimate(flops=20 * tokens * cols, bytes_accessed=6 * tokens * cols, transcendentals=2 * tokens * cols),
        name="row_stats",
    )(targets, policy, refer)


def merge(stats):
    table = jnp.stack(stats)
    peak = jnp.max(table[:, 0], axis=0)
    share = jnp.exp(table[:, 0] - peak)
    total = jnp.sum(share * table[:, 1], axis=0)
    cross = jnp.sum(share * table[:, 2], axis=0)
    ref_peak = jnp.max(table[:, 3], axis=0)
    ref_total = jnp.sum(jnp.exp(table[:, 3] - ref_peak) * table[:, 4], axis=0)
    picked = jnp.sum(table[:, 5], axis=0)
    ref_picked = jnp.sum(table[:, 6], axis=0)
    return jnp.stack([peak, total, cross, ref_peak, ref_total, picked, ref_picked, jnp.zeros_like(peak)])


def grad_body(n_seq, stats_ref, targets_ref, sequence_ref, response_ref, policy_ref, refer_ref, grad_ref, loss_ref):
    tokens, cols = policy_ref.shape
    core_here, x, y, z = where_am_i()
    start_col = (((z * CORES + core_here) * RING + x) * RING + y) * cols
    stats = stats_ref[...]
    peak, total, cross, ref_peak, ref_total, picked, ref_picked = [stats[k : k + 1] for k in range(7)]
    targets, sequence, response = [ref[...].reshape(1, tokens) for ref in (targets_ref, sequence_ref, response_ref)]
    log_total = peak + jnp.log(total)
    ref_log_total = ref_peak + jnp.log(ref_total)
    mean_gap = cross / total
    diverge = mean_gap - log_total + ref_log_total
    mask = response.astype(F32)
    delta = mask * ((picked - log_total) - (ref_picked - ref_log_total))
    ids = lax.broadcasted_iota(jnp.int32, (n_seq, tokens), 0)
    member = (ids == sequence).astype(F32)
    pair = lax.broadcasted_iota(jnp.int32, (n_seq // 2, tokens), 0)
    side = jnp.where(pair == sequence >> 1, jnp.where((sequence & 1) == 0, 1.0, -1.0), 0.0)
    margin = BETA * jnp.sum(side * delta, axis=1, keepdims=True)
    pull = BETA * jax.nn.sigmoid(-margin)
    token_grad = -jnp.sum(side * pull, axis=0, keepdims=True)
    losses = jnp.maximum(-margin, 0.0) + jnp.log1p(jnp.exp(-jnp.abs(margin)))
    objective = jnp.sum(losses) + KL_WEIGHT * jnp.sum(mask * diverge)
    loss_ref[...] = jnp.full(loss_ref.shape, objective / tokens, F32)

    lift = LOSS_SCALE * mask
    local = targets - start_col
    local = jnp.where((local >= 0) & (local < cols), local, -1).astype(F32)
    rows8 = lax.broadcasted_iota(jnp.int32, (128, tokens), 0)
    packed = jnp.zeros((128, tokens), F32)
    for k, value in enumerate((log_total, mean_gap, lift * token_grad, lift * KL_WEIGHT, local)):
        packed = jnp.where(rows8 == k, value, packed)
    packed = packed.T

    step = 128
    pieces = []
    for i in range(tokens // step):
        span = slice(i * step, (i + 1) * step)
        per_row = packed[span]
        policy = policy_ref[span, :]
        refer = in_token_order(refer_ref[span, :], core_here)
        column = lax.broadcasted_iota(jnp.int32, (step, cols), 1)
        hit = (column == per_row[:, 4:5].astype(jnp.int32)).astype(F32)
        probs = jnp.exp(policy - per_row[:, 0:1])
        grad = per_row[:, 2:3] * (hit - probs) + per_row[:, 3:4] * probs * ((policy - refer) - per_row[:, 1:2])
        pieces.append(grad.astype(BF16))
    grad = jnp.concatenate(pieces, axis=0)

    row = lax.broadcasted_iota(jnp.int32, (tokens, tokens), 0)
    token = lax.broadcasted_iota(jnp.int32, (tokens, tokens), 1)
    dx, dy, dz, core, t = row >> 7, (row >> 5) & 3, (row >> 3) & 3, (row >> 2) & 1, row & 3
    source = (z ^ dz) * 128 + core * 64 + (x ^ dx) * 16 + (y ^ dy) * 4 + t
    pick = (token == source).astype(F32).astype(BF16)
    grad_ref[...] = jnp.dot(pick, grad, preferred_element_type=F32).astype(BF16)


def logit_grads(stats, targets, sequence, response, policy, refer, n_seq):
    tokens, cols = policy.shape
    vmem = pl.BlockSpec(memory_space=pltpu.VMEM)
    return pl.pallas_call(
        functools.partial(grad_body, n_seq),
        out_shape=(
            jax.ShapeDtypeStruct((tokens, cols), BF16),
            jax.ShapeDtypeStruct((8, 128), F32),
        ),
        in_specs=[vmem] * 6,
        out_specs=(vmem, vmem),
        compiler_params=params(24),
        cost_estimate=pl.CostEstimate(flops=2 * tokens * tokens * cols, bytes_accessed=10 * tokens * cols, transcendentals=tokens * cols),
        name="logit_grads",
    )(stats, targets, sequence, response, policy, refer)


PARTS = ((True, 1), (True, 3), (False, 1), (False, 3))
SENDS = {1: (1, 2), 3: (3, 2)}
KEEPS = {1: (0, 3), 3: (0, 1)}


def hidden_body(own_grad, other_grad, own_weight, other_weight, *refs):
    outs, (grads, slabs, results, sems) = refs[:8], refs[8:]
    tokens, cols = own_grad.shape
    core = lax.axis_index("dp") & 1
    half = own_weight.shape[0] // CORES
    depth = half // 4
    step = depth // 2
    loads = [
        pltpu.make_async_copy(ref, grads.at[:, pl.ds(i * cols, cols)], sems.at[i])
        for i, ref in enumerate((own_grad, other_grad))
    ]
    fetches = []
    for i in range(8):
        rows = pl.ds(pl.multiple_of(core * half + i * step, step), step)
        fetches.append(
            [
                pltpu.make_async_copy(ref.at[rows], slabs.at[i, :, pl.ds(n * cols, cols)], sems.at[2 + 2 * i + n])
                for n, ref in enumerate((own_weight, other_weight))
            ]
        )
    stores = [pltpu.make_async_copy(results.at[i], outs[i], sems.at[18 + i]) for i in range(8)]
    for copy in loads + sum(fetches, []):
        copy.start()
    for copy in loads:
        copy.wait()
    unit = tokens // CHIPS
    for i in range(8):
        part = i // 2
        along_x, first = PARTS[part]
        for copy in fetches[i]:
            copy.wait()
        product = lax.dot_general(grads[...], slabs[i], (((1,), (1,)), ((), ())), preferred_element_type=F32).astype(BF16)
        for n, order in ((2 * part, SENDS[first]), (2 * part + 1, KEEPS[first])):
            for k, outer in enumerate(order):
                for inner in range(RING):
                    source = (outer * RING + inner) if along_x else (inner * RING + outer)
                    there = (k * RING + inner) * unit
                    results[n, there : there + unit, (i % 2) * step : (i % 2 + 1) * step] = product[
                        source * unit : (source + 1) * unit
                    ]
        if i % 2 == 1:
            stores[2 * part].start()
            stores[2 * part + 1].start()
    for copy in stores:
        copy.wait()


def hidden_parts(own_grad, other_grad, weight, other_weight):
    tokens, cols = own_grad.shape
    depth = weight.shape[0] // CORES // 4
    return pl.pallas_call(
        hidden_body,
        out_shape=(jax.ShapeDtypeStruct((tokens // 2, depth), BF16),) * 8,
        in_specs=[any_spec()] * 4,
        out_specs=(any_spec(),) * 8,
        scratch_shapes=[
            pltpu.VMEM((tokens, CORES * cols), BF16),
            pltpu.VMEM((8, depth // 2, CORES * cols), BF16),
            pltpu.VMEM((8, tokens // 2, depth), BF16),
            pltpu.SemaphoreType.DMA((26,)),
        ],
        compiler_params=params(50),
        cost_estimate=pl.CostEstimate(
            flops=16 * tokens * depth * cols, bytes_accessed=16 * cols * (tokens + depth) + 8 * tokens * depth, transcendentals=0
        ),
        name="hidden_parts",
    )(own_grad, other_grad, weight, other_weight)


def add(*terms):
    total = terms[0].astype(F32)
    for term in terms[1:]:
        total = total + term.astype(F32)
    return total


def shards(hidden, weight, ref_logits, targets, sequence, response):
    rows, width = hidden.shape
    cols = weight.shape[1]
    half = width // CORES
    dp, t = lax.axis_index("dp"), lax.axis_index("tensor")
    z, core = dp // CORES, dp % CORES
    x, y = t // RING, t % RING

    piece = width // CHIPS
    across = [
        lax.dynamic_slice(hidden, (first, (t ^ offset) * piece), (rows // 2, piece))
        for first, offset in ((0, 0), (0, 1), (rows // 2, 0), (rows // 2, RING))
    ]
    across = swap_z(jnp.stack(across), 2)
    sent, across = lax.optimization_barrier((hidden, across))
    near = [swap_z(sent, 1), swap_z(sent, 3)]
    other_weight = swap_core(weight)
    theirs = swap_core(hidden)
    ref_logits = ref_logits.reshape(RING, RING, CORES, CHIPS, cols)
    ref_own, ref_other = [
        lax.dynamic_index_in_dim(ref_logits, c, 2, keepdims=False).transpose(1, 2, 0, 3).reshape(RING * CHIPS, RING, cols)
        for c in (core, 1 - core)
    ]
    ref_other = swap_core(ref_other)
    ref_both = jnp.concatenate([ref_own, ref_other], axis=1)
    by_x, by_y = across[:2], across[2:]
    for step_x, step_y in ((3, 12), (4, 1)):
        by_x = jnp.concatenate([by_x, swap_tensor(by_x, step_x)], axis=0)
        by_y = jnp.concatenate([by_y, swap_tensor(by_y, step_y)], axis=0)
        by_x, by_y = lax.optimization_barrier((by_x, by_y))
    by_x, by_y, other_weight = lax.optimization_barrier((by_x, by_y, other_weight))
    swapped = [swap_core(by_x), swap_core(by_y)]
    late = [swap_tensor(by_x, 12), swap_tensor(by_y, 3)]
    ref_both, swapped = lax.optimization_barrier((ref_both, swapped))
    refer = lax.all_to_all(
        ref_both,
        ("dp", "tensor"),
        split_axis=0,
        concat_axis=0,
        tiled=True,
        axis_index_groups=[
            [(ring * CORES + c) * CHIPS + chip for ring in range(RING) for chip in range(CHIPS)] for c in range(CORES)
        ],
    )
    near, late = lax.optimization_barrier((near, late))
    near += [swap_core(a) for a in near]
    swapped += [swap_core(a) for a in late]
    gathered = [by_x, late[0], by_y, late[1], swapped[0], swapped[2], swapped[1], swapped[3]]
    policy = policy_logits(hidden, theirs, near, gathered, weight)
    refer, policy = lax.optimization_barrier((refer, policy))
    refer = refer.reshape(policy.shape)
    stats = row_stats(targets, policy, refer)

    for send, steps in (
        (swap_tensor, (1, 2, 3)),
        (swap_tensor, (4, 8, 12)),
        (swap_z, (1, 2, 3)),
    ):
        stats = merge([stats] + [send(stats, o) for o in steps])
    stats = merge([stats, swap_core(stats)])

    grad, loss = logit_grads(stats, targets, sequence, response, policy, refer, 2 * RING * CORES)

    sums = {4: [], 1: []}
    products = hidden_parts(grad, swap_core(grad), weight, other_weight)
    for part, (along_x, first) in enumerate(PARTS):
        send, keep = products[2 * part], products[2 * part + 1]
        axis = RING if along_x else 1
        got = swap_tensor(send, axis * first)
        n = keep.shape[0] // 2
        more = swap_tensor(add(keep[n:], got[n:]).astype(BF16), axis * (RING - first))
        sums[axis].append(add(keep[:n], got[:n], more).astype(BF16))
    ends = []
    for axis, cross in ((4, 1), (1, 4)):
        block = jnp.concatenate(sums[axis], axis=1)
        block = block.reshape(RING, block.shape[0] // RING, -1)
        ends.append(add(block[0], *[swap_tensor(block[k], cross * k) for k in (2, 1, 3)]).astype(BF16))
    ends = jnp.concatenate(ends, axis=1).reshape(RING, CORES * RING, half)
    d_half = add(ends[0], *[swap_z(ends[k], k) for k in (2, 1, 3)]).astype(BF16).reshape(CORES, RING, half)
    own_rows = lax.dynamic_index_in_dim(d_half, core, 0, keepdims=False)
    got_rows = swap_core(lax.dynamic_index_in_dim(d_half, 1 - core, 0, keepdims=False))
    d_hidden = jnp.where(
        core == 0, jnp.concatenate([own_rows, got_rows], axis=1), jnp.concatenate([got_rows, own_rows], axis=1)
    )
    return d_hidden, loss[0, 0]


def solution(mesh):
    in_specs = (P("dp", None), P(None, ("dp", "tensor")), P(("dp", "tensor"), None), P(), P(), P())
    out_specs = (P(("dp", "tensor"), None), P())
    return jax.shard_map(shards, mesh=mesh, in_specs=in_specs, out_specs=out_specs, check_vma=False)
```
